256 devices in a mesh: hst: 64 (over z, x, core), tensor: 4 (over y).
Axes of the slice: x: 4, y: 4, z: 8, core: 2. Of those that a mesh axis runs over, the one named last changes fastest.
Arguments:
- query_slots: bfloat16 [64, 64, 8192], P('hst', None, 'tensor'), may hold values from -16 to 16
- keys: bfloat16 [524288, 1024], P('hst', 'tensor'), may hold values from -16 to 16
- values: bfloat16 [524288, 1024], P('hst', 'tensor'), may hold values from -96 to 96
- counts: int32 [64], P('hst'), may hold values from 2048 to 8192, as said below
- query_host: int32 [1], replicated, may hold values from 0 to 63
- out_weight: bfloat16 [8192, 8192], P('tensor', 'hst'), may hold values from -0.0625 to 0.0625
Outputs:
- layer_out: bfloat16 [64, 8192], P('tensor', 'hst')
The draws below stay inside these ranges and needn't reach their ends.
Inputs may be any that keep to these rules, and one draw needn't show every extreme that they name: `counts`: some block is full (8192 valid slots) in every draw.
All inputs are finite; a program needn't handle non-finite values.
Results may differ from the reference program's by a relative error of at most 0.005.
Values may be sent and summed in bfloat16 or wider, within the bound.
No kernel may reach another device: no remote copies, remote signals or barrier semaphores. Data moves between devices by JAX's collectives and lax.ppermute only.
A program may use at most 192 MiB of HBM per device.

```python
import jax
import jax.numpy as jnp
from jax import lax

D = 8192
QUERY_HEADS = 64
KEY_VALUE_HEADS = 8
HEAD_SIZE = 128
QUERY_TOKENS = 64
BLOCK_SLOTS = 8192
CONTEXT_SLOTS = 524288
N_HST = 64


def common_keys(key):
    return jax.random.normal(key, (CONTEXT_SLOTS, KEY_VALUE_HEADS * HEAD_SIZE), jnp.float32)


def draw_keys(key, part):
    base_offset = common_keys(key)
    return jnp.clip(base_offset, -6.0, 6.0).astype(jnp.bfloat16)


def draw_query_slots(key, part):
    key = jax.random.fold_in(key, 5)
    noise = jax.random.normal(key, (N_HST, QUERY_TOKENS, QUERY_HEADS * HEAD_SIZE), jnp.float32) * 3.0
    return jnp.clip(noise, -16.0, 16.0).astype(jnp.bfloat16)


def draw_counts(key, part):
    key = jax.random.fold_in(key, 7)
    first_key, second_key = jax.random.split(key)
    result = jax.random.randint(first_key, (N_HST,), BLOCK_SLOTS // 4, BLOCK_SLOTS + 1, jnp.int32)
    full_block = jax.random.randint(second_key, (), 0, N_HST, jnp.int32)
    return result.at[full_block].set(BLOCK_SLOTS).astype(jnp.int32)


def shard_levels(rng, dims, pieces, low, top_value):
    def one(axis_at, shards_of):
        heights = jax.random.uniform(jax.random.fold_in(jax.random.fold_in(rng, 6), axis_at), (shards_of,), jnp.float32, low / len(pieces), top_value / len(pieces))
        return jnp.repeat(jnp.exp(heights), dims[axis_at] // shards_of).reshape((-1,) + (1,) * (len(dims) - axis_at - 1))

    gain = one(*pieces[0])
    for cut in pieces[1:]:
        gain = gain * one(*cut)
    return gain


def normal_values(rng, extent, deviation, limit, cuts=(), held_as=jnp.bfloat16):
    values = jax.random.normal(rng, extent, jnp.float32) * deviation
    if len(cuts) > 0:
        values = shard_levels(rng, extent, cuts, -0.22, 0.18) * values
    return jnp.clip(values, min=-limit, max=limit).astype(held_as)


def setup_inputs(seed: int = 0) -> dict:
    splits = jax.random.split(jax.random.key(seed), 7)
    query_slots = draw_query_slots(jax.random.fold_in(splits[6], 71), 0)
    keys = draw_keys(jax.random.fold_in(splits[6], 71), 0)
    values = normal_values(splits[2], (CONTEXT_SLOTS, KEY_VALUE_HEADS * HEAD_SIZE), 16.0, 96.0, ((0, 64), (1, 4)))
    counts = draw_counts(jax.random.fold_in(splits[6], 71), 0)
    query_host = jax.random.randint(splits[4], (1,), 0, N_HST).astype(jnp.int32)
    out_weight = normal_values(splits[5], (QUERY_HEADS * HEAD_SIZE, D), (QUERY_HEADS * HEAD_SIZE) ** -0.5, 0.0625, ((0, 4), (1, 64)))
    return {"query_slots": query_slots, "keys": keys, "values": values, "counts": counts, "query_host": query_host, "out_weight": out_weight}


def reference(query_slots, keys, values, counts, query_host, out_weight):
    root_host = query_host[0].astype(jnp.int32)
    query_tokens = lax.dynamic_index_in_dim(query_slots, root_host, 0, keepdims=False)
    query_group_size = QUERY_HEADS // KEY_VALUE_HEADS
    score_scale = HEAD_SIZE ** -0.5
    query_head_count = query_tokens.astype(jnp.float32).reshape(QUERY_TOKENS, KEY_VALUE_HEADS, query_group_size, HEAD_SIZE)

    def one_block(block_index):
        start_slot = (block_index * BLOCK_SLOTS).astype(jnp.int32)
        host_block_keys = lax.dynamic_slice_in_dim(keys, start_slot, BLOCK_SLOTS, 0).astype(jnp.float32).reshape(BLOCK_SLOTS, KEY_VALUE_HEADS, HEAD_SIZE)
        host_block_values = lax.dynamic_slice_in_dim(values, start_slot, BLOCK_SLOTS, 0).astype(jnp.float32).reshape(BLOCK_SLOTS, KEY_VALUE_HEADS, HEAD_SIZE)
        valid_count = counts[block_index]
        key_limit = jnp.where(block_index == root_host, valid_count - QUERY_TOKENS + 1 + jnp.arange(QUERY_TOKENS, dtype=jnp.int32), valid_count)
        visible = jnp.arange(BLOCK_SLOTS, dtype=jnp.int32)[None, :] < key_limit[:, None]
        scores = jnp.einsum("qhgd,khd->hgqk", query_head_count, host_block_keys) * score_scale
        scores = jnp.where(visible[None, None], scores, -1e30)
        row_max = jnp.max(scores, axis=-1)
        weights = jnp.exp(scores - row_max[..., None])
        row_sum = jnp.sum(weights, axis=-1)
        weights_bf = lax.optimization_barrier(weights.astype(jnp.bfloat16)).astype(jnp.float32)
        partial_value = jnp.einsum("hgqk,khd->hgqd", weights_bf, host_block_values)
        return row_max, row_sum, partial_value

    maxima, sums, partials = lax.map(one_block, jnp.arange(N_HST, dtype=jnp.int32))
    peak_score = jnp.max(maxima, axis=0)
    factors = jnp.exp(maxima - peak_score)
    totals = jnp.sum(sums * factors, axis=0)
    merged = jnp.sum(partials * factors[..., None], axis=0)
    attended = (merged / totals[..., None]).astype(jnp.bfloat16)
    attended = attended.transpose(2, 0, 1, 3).reshape(QUERY_TOKENS, QUERY_HEADS * HEAD_SIZE)
    return jnp.dot(attended, out_weight, preferred_element_type=jnp.float32).astype(jnp.bfloat16)
```

```python
import jax
import jax.numpy as jnp
from jax import lax
from jax.experimental import pallas as pl
from jax.experimental.pallas import tpu as pltpu
from jax.sharding import PartitionSpec as P

HEAD_SIZE = 128
PIECE = 16
CHUNK = 1024
LOG2E = 1.4426950408889634
SCORE_SCALE = LOG2E * HEAD_SIZE ** (-0.5)
MASKED = -1e30
VMEM = pl.BlockSpec(memory_space=pltpu.VMEM)
SMEM = pl.BlockSpec(memory_space=pltpu.SMEM)


def dot(lhs, rhs, lhs_dim, rhs_dim):
    return lax.dot_general(
        lhs, rhs, (((lhs_dim,), (rhs_dim,)), ((), ())), preferred_element_type=jnp.float32
    )


def attend_kernel(limits_ref, queries_ref, keys_ref, values_ref, packed_ref, row_max, sums):
    block_len = keys_ref.shape[0]
    kv_heads = keys_ref.shape[1] // HEAD_SIZE
    rows = queries_ref.shape[0] // kv_heads
    tokens = limits_ref[2]
    first_limit = limits_ref[0]
    last_limit = limits_ref[1]
    row_max[...] = jnp.full_like(row_max, MASKED)
    sums[...] = jnp.zeros_like(sums)

    def step(chunk, masked):
        base = pl.multiple_of(chunk * CHUNK, CHUNK)
        for head in range(kv_heads):
            columns = slice(head * HEAD_SIZE, (head + 1) * HEAD_SIZE)
            keys = keys_ref[pl.ds(base, CHUNK), columns]
            values = values_ref[pl.ds(base, CHUNK), columns]
            scores = dot(keys, queries_ref[head * rows : (head + 1) * rows], 1, 1) * SCORE_SCALE
            if masked:
                token = lax.rem(lax.broadcasted_iota(jnp.int32, (1, rows), 1), tokens)
                limit = jnp.minimum(first_limit + token, last_limit)
                slot = lax.broadcasted_iota(jnp.int32, scores.shape, 0) + base
                scores = jnp.where(slot < limit, scores, MASKED)
            before = row_max[head]
            now = jnp.maximum(before, jnp.max(scores, axis=0, keepdims=True))
            weights = jnp.exp2(scores - now).astype(jnp.bfloat16)
            lhs = jnp.concatenate([values.T, jnp.ones((16, CHUNK), jnp.bfloat16)], axis=0)
            sums[head] = sums[head] * jnp.exp2(before - now) + dot(lhs, weights, 1, 0)
            row_max[head] = now

    whole = first_limit // CHUNK
    lax.fori_loop(0, whole, lambda chunk, _: (step(chunk, False), 0)[1], 0)
    lax.fori_loop(whole, pl.cdiv(last_limit, CHUNK), lambda chunk, _: (step(chunk, True), 0)[1], 0)

    pieces = rows // PIECE
    row = lax.broadcasted_iota(jnp.int32, (pieces, PIECE, HEAD_SIZE), 1)
    lane = lax.broadcasted_iota(jnp.int32, (pieces, PIECE, HEAD_SIZE), 2)
    for head in range(kv_heads):
        total = sums[head, HEAD_SIZE : HEAD_SIZE + 1]
        out = (sums[head, :HEAD_SIZE] / total).T.astype(jnp.bfloat16)
        rounded_max = row_max[head].astype(jnp.bfloat16).astype(jnp.float32)
        total = total * jnp.exp2(row_max[head] - rounded_max)
        high = total.astype(jnp.bfloat16).astype(jnp.float32)

        def spread(value):
            return jnp.broadcast_to(value, (HEAD_SIZE, rows)).T.reshape(pieces, PIECE, HEAD_SIZE)

        stats = jnp.where(lane == row, spread(rounded_max), 0.0)
        stats = jnp.where(lane == row + PIECE, spread(high), stats)
        stats = jnp.where(lane == row + 2 * PIECE, spread(total - high), stats)
        stats = jnp.sum(stats, axis=1, keepdims=True).astype(jnp.bfloat16)
        where = slice(head * pieces, (head + 1) * pieces)
        packed_ref[where, :PIECE] = out.reshape(pieces, PIECE, HEAD_SIZE)
        packed_ref[where, PIECE:] = jnp.broadcast_to(stats, (pieces, 8, HEAD_SIZE))


def merge_kernel(packed_ref, attended_ref):
    hosts = packed_ref.shape[0]
    stats = jnp.max(packed_ref[:, PIECE:].astype(jnp.float32), axis=1).T
    row_max = stats[:PIECE]
    totals = stats[PIECE : 2 * PIECE] + stats[2 * PIECE : 3 * PIECE]
    peak = jnp.max(row_max, axis=1, keepdims=True)
    shares = totals * jnp.exp2(row_max - peak)
    shares = shares / jnp.sum(shares, axis=1, keepdims=True)
    merged = jnp.zeros((PIECE, HEAD_SIZE), jnp.float32)
    for host in range(hosts):
        merged += shares[:, host : host + 1] * packed_ref[host, :PIECE].astype(jnp.float32)
    attended_ref[...] = jnp.broadcast_to(
        merged.astype(jnp.bfloat16)[None], attended_ref.shape
    )


def project_kernel(attended_ref, weight_ref, out_ref):
    per_head = out_ref.shape[0]
    heads = attended_ref.shape[0] // per_head
    total = None
    for head in range(0, heads, 2):
        pair = [
            attended_ref[(head + k) * per_head : (head + k + 1) * per_head].reshape(-1, HEAD_SIZE)
            for k in range(2)
        ]
        part = dot(
            jnp.concatenate(pair, axis=1),
            weight_ref[head * HEAD_SIZE : (head + 2) * HEAD_SIZE],
            1,
            0,
        )
        total = part if total is None else total + part
    out_ref[...] = total.reshape(out_ref.shape)


def kernel_call(body, out_shape, in_specs, scratch=(), flops=0, name=None):
    return pl.pallas_call(
        body,
        out_shape=out_shape,
        in_specs=in_specs,
        out_specs=VMEM,
        scratch_shapes=scratch,
        compiler_params=pltpu.CompilerParams(vmem_limit_bytes=40 << 20),
        name=name,
    )


def on_device(query_slots, keys, values, counts, query_host, out_weight):
    tokens, width = query_slots.shape[1:]
    heads = width // HEAD_SIZE
    kv_heads = keys.shape[1] // HEAD_SIZE
    rows = heads // kv_heads * tokens
    groups = tokens // PIECE
    pieces = heads * groups
    root = query_host[0]

    with jax.named_scope("queries"):
        slots = (
            query_slots[0]
            .reshape(groups, PIECE, heads, HEAD_SIZE)
            .transpose(2, 0, 1, 3)
            .reshape(pieces, PIECE, HEAD_SIZE)
        )
        received = lax.all_to_all(slots, "hst", 0, 0)
        served = lax.dynamic_index_in_dim(received, root, 0)
        queries = lax.all_to_all(jnp.broadcast_to(served, slots.shape), "hst", 0, 0)
        queries = queries.reshape(pieces * PIECE, HEAD_SIZE)

    with jax.named_scope("attend"):
        last = counts[0]
        first = jnp.where(lax.axis_index("hst") == root, last - tokens + 1, last)
        limits = jnp.stack([first, last, jnp.int32(tokens)])
        packed = kernel_call(
            attend_kernel,
            jax.ShapeDtypeStruct((pieces, PIECE + 8, HEAD_SIZE), jnp.bfloat16),
            [SMEM, VMEM, VMEM, VMEM],
            [
                pltpu.VMEM((kv_heads, 1, rows), jnp.float32),
                pltpu.VMEM((kv_heads, HEAD_SIZE + 16, rows), jnp.float32),
            ],
            name="attend",
        )(limits, queries, keys, values)

    with jax.named_scope("merge"):
        packed = lax.all_to_all(packed, "hst", 0, 0)
        attended = kernel_call(
            merge_kernel,
            jax.ShapeDtypeStruct((pieces, PIECE, HEAD_SIZE), jnp.bfloat16),
            [VMEM],
            name="merge",
        )(packed)
        attended = lax.all_to_all(attended, "hst", 0, 0)

    with jax.named_scope("project"):
        projected = kernel_call(
            project_kernel,
            jax.ShapeDtypeStruct((groups, PIECE, out_weight.shape[1]), jnp.float32),
            [VMEM, VMEM],
            name="project",
        )(attended, out_weight)
        n = lax.axis_size("tensor")
        mine = lax.axis_index("tensor")
        total = lax.dynamic_index_in_dim(projected, mine, 0, keepdims=False)
        for hop in range(1, n):
            part = lax.dynamic_index_in_dim(projected, (mine + hop) % n, 0, keepdims=False)
            total += lax.ppermute(part, "tensor", [(i, (i + hop) % n) for i in range(n)])
        return total.astype(jnp.bfloat16)


def solution(mesh):
    placed = (
        P("hst", None, "tensor"),
        P("hst", "tensor"),
        P("hst", "tensor"),
        P("hst"),
        P(),
        P("tensor", "hst"),
    )
    return jax.shard_map(
        on_device, mesh=mesh, in_specs=placed, out_specs=P("tensor", "hst"), check_vma=False
    )
```

```python
import jax
import jax.numpy as jnp
from jax import lax
from jax.experimental import pallas as pl
from jax.experimental.pallas import tpu as pltpu
from jax.sharding import PartitionSpec as P

HEAD_SIZE = 128
PIECE = 16
CHUNK = 1024
LOG2E = 1.4426950408889634
SCORE_SCALE = LOG2E * HEAD_SIZE ** (-0.5)
MASKED = -1e30
SAMPLE = 128
SUM_LIMIT = 2.0**64
Z, X, CORES = 8, 4, 2
HBM = pl.BlockSpec(memory_space=pl.ANY)
VMEM = pl.BlockSpec(memory_space=pltpu.VMEM)
SMEM = pl.BlockSpec(memory_space=pltpu.SMEM)


def dot(lhs, rhs, lhs_dim, rhs_dim):
    return lax.dot_general(
        lhs, rhs, (((lhs_dim,), (rhs_dim,)), ((), ())), preferred_element_type=jnp.float32
    )


def attend_kernel(
    scalars_ref, queries_ref, keys_hbm, values_hbm, packed_ref,
    queries, keys_ref, values_ref, row_max, sums, arrivals,
):
    block_len, width = keys_ref.shape
    kv_heads = width // HEAD_SIZE
    cores, stretches, tokens, columns = queries_ref.shape
    rows = queries.shape[1]
    first_limit = scalars_ref[0]
    last_limit = scalars_ref[1]
    my_core = scalars_ref[2]
    my_x = scalars_ref[3]
    chunks = pl.cdiv(last_limit, CHUNK)

    def copies(chunk):
        place = pl.ds(pl.multiple_of(chunk * CHUNK, CHUNK), CHUNK)
        return (
            pltpu.make_async_copy(keys_hbm.at[place], keys_ref.at[place], arrivals.at[0, chunk]),
            pltpu.make_async_copy(values_hbm.at[place], values_ref.at[place], arrivals.at[1, chunk]),
        )

    def fetch(chunk, carry):
        for copy in copies(chunk):
            copy.start()
        return carry

    lax.fori_loop(0, chunks, fetch, 0)

    per_piece = columns // HEAD_SIZE
    for stretch in range(stretches):
        for core in range(cores):
            piece = queries_ref[
                jnp.where(my_core == core, 0, 1), lax.rem(my_x - stretch + stretches, stretches)
            ]
            for part in range(per_piece):
                head = (stretch * cores + core) * per_piece + part
                queries[head * tokens // rows, pl.ds(head * tokens % rows, tokens)] = piece[
                    :, part * HEAD_SIZE : (part + 1) * HEAD_SIZE
                ]
    sums[...] = jnp.zeros_like(sums)

    def scores_of(base, count, head):
        keys = keys_ref[pl.ds(base, count), head * HEAD_SIZE : (head + 1) * HEAD_SIZE]
        return dot(keys, queries[head], 1, 1) * SCORE_SCALE

    def step(chunk, masked, running):
        base = pl.multiple_of(chunk * CHUNK, CHUNK)
        for head in range(kv_heads):
            scores = scores_of(base, CHUNK, head)
            if masked:
                token = lax.rem(lax.broadcasted_iota(jnp.int32, (1, rows), 1), tokens)
                limit = jnp.minimum(first_limit + token, last_limit)
                slot = lax.broadcasted_iota(jnp.int32, scores.shape, 0) + base
                scores = jnp.where(slot < limit, scores, MASKED)
            if running:
                before = row_max[head]
                row_max[head] = jnp.maximum(before, jnp.max(scores, axis=0, keepdims=True))
                sums[head] *= jnp.exp2(before - row_max[head])
            weights = jnp.exp2(scores - row_max[head]).astype(jnp.bfloat16)
            values = values_ref[pl.ds(base, CHUNK), head * HEAD_SIZE : (head + 1) * HEAD_SIZE]
            lhs = jnp.concatenate([values.T, jnp.ones((16, CHUNK), jnp.bfloat16)], axis=0)
            sums[head] += dot(lhs, weights, 1, 0)

    def arrived_step(chunk, masked):
        for copy in copies(chunk):
            copy.wait()
        step(chunk, masked, False)

    def loop(start, stop, body):
        def one(chunk, carry):
            body(chunk)
            return carry

        lax.fori_loop(start, stop, one, 0)

    whole = first_limit // CHUNK
    first_keys, first_values = copies(0)
    first_keys.wait()
    for head in range(kv_heads):
        row_max[head] = jnp.max(scores_of(0, SAMPLE, head), axis=0, keepdims=True)
    first_values.wait()
    step(0, False, False)
    loop(1, whole, lambda chunk: arrived_step(chunk, False))
    loop(whole, chunks, lambda chunk: arrived_step(chunk, True))

    fits = jnp.where(sums[:, HEAD_SIZE : HEAD_SIZE + 1] < SUM_LIMIT, 0, 1)

    @pl.when(jnp.sum(fits) > 0)
    def _():
        row_max[...] = jnp.full_like(row_max, MASKED)
        sums[...] = jnp.zeros_like(sums)
        loop(0, chunks, lambda chunk: step(chunk, True, True))

    pieces = rows // PIECE
    row = lax.broadcasted_iota(jnp.int32, (pieces, PIECE, HEAD_SIZE), 1)
    lane = lax.broadcasted_iota(jnp.int32, (pieces, PIECE, HEAD_SIZE), 2)
    for head in range(kv_heads):
        total = sums[head, HEAD_SIZE : HEAD_SIZE + 1]
        out = (sums[head, :HEAD_SIZE] / total).T.astype(jnp.bfloat16)
        rounded_max = row_max[head].astype(jnp.bfloat16).astype(jnp.float32)
        total = total * jnp.exp2(row_max[head] - rounded_max)
        high = total.astype(jnp.bfloat16).astype(jnp.float32)

        def spread(value):
            return jnp.broadcast_to(value, (HEAD_SIZE, rows)).T.reshape(pieces, PIECE, HEAD_SIZE)

        stats = jnp.where(lane == row, spread(rounded_max), 0.0)
        stats = jnp.where(lane == row + PIECE, spread(high), stats)
        stats = jnp.where(lane == row + 2 * PIECE, spread(total - high), stats)
        stats = jnp.sum(stats, axis=1, keepdims=True).astype(jnp.bfloat16)
        where = slice(head * pieces, (head + 1) * pieces)
        packed_ref[where, :PIECE] = out.reshape(pieces, PIECE, HEAD_SIZE)
        packed_ref[where, PIECE:] = jnp.broadcast_to(stats, (pieces, 8, HEAD_SIZE))


def merge_kernel(packed_ref, attended_ref):
    hosts = packed_ref.shape[0]
    stats = jnp.max(packed_ref[:, PIECE:].astype(jnp.float32), axis=1).T
    row_max = stats[:PIECE]
    totals = stats[PIECE : 2 * PIECE] + stats[2 * PIECE : 3 * PIECE]
    peak = jnp.max(row_max, axis=1, keepdims=True)
    shares = totals * jnp.exp2(row_max - peak)
    shares = shares / jnp.sum(shares, axis=1, keepdims=True)
    merged = jnp.zeros((PIECE, HEAD_SIZE), jnp.float32)
    for host in range(hosts):
        merged += shares[:, host : host + 1] * packed_ref[host, :PIECE].astype(jnp.float32)
    attended_ref[...] = jnp.broadcast_to(
        merged.astype(jnp.bfloat16)[None], attended_ref.shape
    )


def project_kernel(attended_ref, weight_ref, out_ref):
    per_head = out_ref.shape[0]
    heads = attended_ref.shape[0] // per_head
    total = None
    for head in range(0, heads, 2):
        pair = [
            attended_ref[(head + k) * per_head : (head + k + 1) * per_head].reshape(-1, HEAD_SIZE)
            for k in range(2)
        ]
        part = dot(
            jnp.concatenate(pair, axis=1),
            weight_ref[head * HEAD_SIZE : (head + 2) * HEAD_SIZE],
            1,
            0,
        )
        total = part if total is None else total + part
    out_ref[...] = total.reshape(out_ref.shape)


def kernel_call(body, out_shape, in_specs, scratch=(), name=None):
    return pl.pallas_call(
        body,
        out_shape=out_shape,
        in_specs=in_specs,
        out_specs=VMEM,
        scratch_shapes=scratch,
        compiler_params=pltpu.CompilerParams(vmem_limit_bytes=40 << 20),
        name=name,
    )


def shift(value, dz, dx, dcore):
    def index(z, x, core):
        return ((z % Z) * X + x % X) * CORES + core % CORES

    pairs = [
        (index(z, x, core), index(z + dz, x + dx, core + dcore))
        for z in range(Z)
        for x in range(X)
        for core in range(CORES)
    ]
    return lax.ppermute(value, "hst", pairs)


def broadcast_queries(slots, root):
    me = lax.axis_index("hst")
    core, x, z = me % CORES, me // CORES % X, me // (CORES * X)
    root_core, root_x, root_z = root % CORES, root // CORES % X, root // (CORES * X)
    tokens, width = slots.shape
    part = width // (X * CORES)
    parts = slots.reshape(tokens, X, CORES, part).transpose(2, 1, 0, 3)
    own = lax.dynamic_index_in_dim(parts, core, 0, keepdims=False)
    other = shift(lax.dynamic_index_in_dim(parts, 1 - core, 0, keepdims=False), 0, 0, 1)
    half = jnp.where(core == root_core, own, other)

    stretch = lax.dynamic_index_in_dim(half, x, 0, keepdims=False)
    for hop in range(1, X):
        sent = lax.dynamic_index_in_dim(half, (x + hop) % X, 0, keepdims=False)
        stretch = jnp.where((x - root_x) % X == hop, shift(sent, 0, hop, 0), stretch)

    distance = (z - root_z) % Z
    up, down = shift(stretch, 3, 0, 0), shift(stretch, -3, 0, 0)
    stretch = jnp.where(distance == 3, up, jnp.where(distance == 5, down, stretch))
    up, down = shift(stretch, 1, 0, 0), shift(stretch, -1, 0, 0)
    from_below = (distance == 1) | (distance == 4) | (distance == 6)
    from_above = (distance == 2) | (distance == 7)
    stretch = jnp.where(from_below, up, jnp.where(from_above, down, stretch))

    half = jnp.stack([stretch] + [shift(stretch, 0, hop, 0) for hop in range(1, X)])
    return jnp.stack([half, shift(half, 0, 0, 1)])


def on_device(query_slots, keys, values, counts, query_host, out_weight):
    tokens, width = query_slots.shape[1:]
    heads = width // HEAD_SIZE
    kv_heads = keys.shape[1] // HEAD_SIZE
    rows = heads // kv_heads * tokens
    groups = tokens // PIECE
    pieces = heads * groups
    root = query_host[0]

    with jax.named_scope("queries"):
        queries = broadcast_queries(query_slots[0], root)

    with jax.named_scope("attend"):
        me = lax.axis_index("hst")
        last = counts[0]
        first = jnp.where(me == root, last - tokens + 1, last)
        scalars = jnp.stack([first, last, me % CORES, me // CORES % X])
        packed = kernel_call(
            attend_kernel,
            jax.ShapeDtypeStruct((pieces, PIECE + 8, HEAD_SIZE), jnp.bfloat16),
            [SMEM, VMEM, HBM, HBM],
            [
                pltpu.VMEM((kv_heads, rows, HEAD_SIZE), jnp.bfloat16),
                pltpu.VMEM(keys.shape, jnp.bfloat16),
                pltpu.VMEM(values.shape, jnp.bfloat16),
                pltpu.VMEM((kv_heads, 1, rows), jnp.float32),
                pltpu.VMEM((kv_heads, HEAD_SIZE + 16, rows), jnp.float32),
                pltpu.SemaphoreType.DMA((2, keys.shape[0] // CHUNK)),
            ],
            name="attend",
        )(scalars, queries, keys, values)

    with jax.named_scope("merge"):
        packed = lax.all_to_all(packed, "hst", 0, 0)
        attended = kernel_call(
            merge_kernel,
            jax.ShapeDtypeStruct((pieces, PIECE, HEAD_SIZE), jnp.bfloat16),
            [VMEM],
            name="merge",
        )(packed)
        attended = lax.all_to_all(attended, "hst", 0, 0)

    with jax.named_scope("project"):
        projected = kernel_call(
            project_kernel,
            jax.ShapeDtypeStruct((groups, PIECE, out_weight.shape[1]), jnp.float32),
            [VMEM, VMEM],
            name="project",
        )(attended, out_weight)
        n = lax.axis_size("tensor")
        mine = lax.axis_index("tensor")
        total = lax.dynamic_index_in_dim(projected, mine, 0, keepdims=False)
        for hop in range(1, n):
            part = lax.dynamic_index_in_dim(projected, (mine + hop) % n, 0, keepdims=False)
            total += lax.ppermute(part, "tensor", [(i, (i + hop) % n) for i in range(n)])
        return total.astype(jnp.bfloat16)


def solution(mesh):
    placed = (
        P("hst", None, "tensor"),
        P("hst", "tensor"),
        P("hst", "tensor"),
        P("hst"),
        P(),
        P("tensor", "hst"),
    )
    return jax.shard_map(
        on_device, mesh=mesh, in_specs=placed, out_specs=P("tensor", "hst"), check_vma=False
    )
```

```python
import jax
import jax.numpy as jnp
from jax import lax
from jax.experimental import pallas as pl
from jax.experimental.pallas import tpu as pltpu
from jax.sharding import PartitionSpec as P

HEAD_SIZE = 128
PIECE = 16
CHUNK = 1024
LOG2E = 1.4426950408889634
SCORE_SCALE = LOG2E * HEAD_SIZE ** (-0.5)
MASKED = -1e30
SAMPLE = 128
SUM_LIMIT = 2.0**64
Z, X, CORES = 8, 4, 2
HBM = pl.BlockSpec(memory_space=pl.ANY)
VMEM = pl.BlockSpec(memory_space=pltpu.VMEM)
SMEM = pl.BlockSpec(memory_space=pltpu.SMEM)


def dot(lhs, rhs, lhs_dim, rhs_dim):
    return lax.dot_general(
        lhs, rhs, (((lhs_dim,), (rhs_dim,)), ((), ())), preferred_element_type=jnp.float32
    )


def attend_kernel(
    scalars_ref, queries_ref, keys_hbm, values_hbm, packed_ref,
    queries, keys_ref, values_ref, row_max, sums, arrivals,
):
    block_len, width = keys_ref.shape
    kv_heads = width // HEAD_SIZE
    cores, groups, _, columns = queries_ref.shape
    tokens = groups * PIECE
    rows = queries.shape[1]
    first_limit = scalars_ref[0]
    last_limit = scalars_ref[1]
    my_core = scalars_ref[2]
    my_x = scalars_ref[3]
    chunks = pl.cdiv(last_limit, CHUNK)

    def copies(chunk):
        place = pl.ds(pl.multiple_of(chunk * CHUNK, CHUNK), CHUNK)
        return (
            pltpu.make_async_copy(keys_hbm.at[place], keys_ref.at[place], arrivals.at[0, chunk]),
            pltpu.make_async_copy(values_hbm.at[place], values_ref.at[place], arrivals.at[1, chunk]),
        )

    def fetch(chunk, carry):
        for copy in copies(chunk):
            copy.start()
        return carry

    lax.fori_loop(0, chunks, fetch, 0)

    per_piece = columns // HEAD_SIZE
    for core in range(cores):
        for group in range(groups):
            piece = queries_ref[
                jnp.where(my_core == core, 0, 1), lax.rem(my_x - group + groups, groups)
            ]
            for part in range(per_piece):
                head = core * per_piece + part
                start = (head * groups + group) * PIECE
                queries[start // rows, pl.ds(start % rows, PIECE)] = piece[
                    :, part * HEAD_SIZE : (part + 1) * HEAD_SIZE
                ]
    sums[...] = jnp.zeros_like(sums)

    def scores_of(base, count, head):
        keys = keys_ref[pl.ds(base, count), head * HEAD_SIZE : (head + 1) * HEAD_SIZE]
        return dot(keys, queries[head], 1, 1) * SCORE_SCALE

    def step(chunk, masked, running):
        base = pl.multiple_of(chunk * CHUNK, CHUNK)
        for head in range(kv_heads):
            scores = scores_of(base, CHUNK, head)
            if masked:
                token = lax.rem(lax.broadcasted_iota(jnp.int32, (1, rows), 1), tokens)
                limit = jnp.minimum(first_limit + token, last_limit)
                slot = lax.broadcasted_iota(jnp.int32, scores.shape, 0) + base
                scores = jnp.where(slot < limit, scores, MASKED)
            if running:
                before = row_max[head]
                row_max[head] = jnp.maximum(before, jnp.max(scores, axis=0, keepdims=True))
                sums[head] *= jnp.exp2(before - row_max[head])
            weights = jnp.exp2(scores - row_max[head]).astype(jnp.bfloat16)
            values = values_ref[pl.ds(base, CHUNK), head * HEAD_SIZE : (head + 1) * HEAD_SIZE]
            lhs = jnp.concatenate([values.T, jnp.ones((16, CHUNK), jnp.bfloat16)], axis=0)
            sums[head] += dot(lhs, weights, 1, 0)

    def arrived_step(chunk, masked):
        for copy in copies(chunk):
            copy.wait()
        step(chunk, masked, False)

    def loop(start, stop, body):
        def one(chunk, carry):
            body(chunk)
            return carry

        lax.fori_loop(start, stop, one, 0)

    whole = first_limit // CHUNK
    first_keys, first_values = copies(0)
    first_keys.wait()
    for head in range(kv_heads):
        row_max[head] = jnp.max(scores_of(0, SAMPLE, head), axis=0, keepdims=True)
    first_values.wait()
    step(0, False, False)
    loop(1, whole, lambda chunk: arrived_step(chunk, False))
    loop(whole, chunks, lambda chunk: arrived_step(chunk, True))

    fits = jnp.where(sums[:, HEAD_SIZE : HEAD_SIZE + 1] < SUM_LIMIT, 0, 1)

    @pl.when(jnp.sum(fits) > 0)
    def _():
        row_max[...] = jnp.full_like(row_max, MASKED)
        sums[...] = jnp.zeros_like(sums)
        loop(0, chunks, lambda chunk: step(chunk, True, True))

    pieces = rows // PIECE
    row = lax.broadcasted_iota(jnp.int32, (pieces, PIECE, HEAD_SIZE), 1)
    lane = lax.broadcasted_iota(jnp.int32, (pieces, PIECE, HEAD_SIZE), 2)
    for head in range(kv_heads):
        total = sums[head, HEAD_SIZE : HEAD_SIZE + 1]
        out = (sums[head, :HEAD_SIZE] / total).T.astype(jnp.bfloat16)
        rounded_max = row_max[head].astype(jnp.bfloat16).astype(jnp.float32)
        total = total * jnp.exp2(row_max[head] - rounded_max)
        high = total.astype(jnp.bfloat16).astype(jnp.float32)

        def spread(value):
            return jnp.broadcast_to(value, (HEAD_SIZE, rows)).T.reshape(pieces, PIECE, HEAD_SIZE)

        stats = jnp.where(lane == row, spread(rounded_max), 0.0)
        stats = jnp.where(lane == row + PIECE, spread(high), stats)
        stats = jnp.where(lane == row + 2 * PIECE, spread(total - high), stats)
        stats = jnp.sum(stats, axis=1, keepdims=True).astype(jnp.bfloat16)
        where = slice(head * pieces, (head + 1) * pieces)
        packed_ref[where, :PIECE] = out.reshape(pieces, PIECE, HEAD_SIZE)
        packed_ref[where, PIECE:] = jnp.broadcast_to(stats, (pieces, 8, HEAD_SIZE))


def merge_kernel(packed_ref, attended_ref):
    hosts = packed_ref.shape[0]
    stats = jnp.max(packed_ref[:, PIECE:].astype(jnp.float32), axis=1).T
    row_max = stats[:PIECE]
    totals = stats[PIECE : 2 * PIECE] + stats[2 * PIECE : 3 * PIECE]
    peak = jnp.max(row_max, axis=1, keepdims=True)
    shares = totals * jnp.exp2(row_max - peak)
    shares = shares / jnp.sum(shares, axis=1, keepdims=True)
    merged = jnp.zeros((PIECE, HEAD_SIZE), jnp.float32)
    for host in range(hosts):
        merged += shares[:, host : host + 1] * packed_ref[host, :PIECE].astype(jnp.float32)
    attended_ref[...] = jnp.broadcast_to(
        merged.astype(jnp.bfloat16)[None], attended_ref.shape
    )


def project_kernel(scalars_ref, own_ref, sibling_ref, weight_ref, out_ref):
    per_head = out_ref.shape[0]
    heads = own_ref.shape[0] * CORES // per_head
    on_first = scalars_ref[2] == 0
    own, sibling = own_ref[...], sibling_ref[...]
    first = jnp.where(on_first, own, sibling)
    second = jnp.where(on_first, sibling, own)
    pieces = [(first, second)[piece % 2][piece // 2] for piece in range(heads * per_head)]
    total = None
    for head in range(0, heads, 2):
        pair = [
            jnp.concatenate(pieces[(head + k) * per_head : (head + k + 1) * per_head], axis=0)
            for k in range(2)
        ]
        part = dot(
            jnp.concatenate(pair, axis=1),
            weight_ref[head * HEAD_SIZE : (head + 2) * HEAD_SIZE],
            1,
            0,
        )
        total = part if total is None else total + part
    out_ref[...] = total.reshape(out_ref.shape)


def kernel_call(body, out_shape, in_specs, scratch=(), vmem=40, name=None):
    return pl.pallas_call(
        body,
        out_shape=out_shape,
        in_specs=in_specs,
        out_specs=VMEM,
        scratch_shapes=scratch,
        compiler_params=pltpu.CompilerParams(vmem_limit_bytes=vmem << 20),
        name=name,
    )


def shift(value, dz, dx, dcore):
    def index(z, x, core):
        return ((z % Z) * X + x % X) * CORES + core % CORES

    pairs = [
        (index(z, x, core), index(z + dz, x + dx, core + dcore))
        for z in range(Z)
        for x in range(X)
        for core in range(CORES)
    ]
    return lax.ppermute(value, "hst", pairs)


def gather(value, groups):
    copies = jnp.broadcast_to(value[None], (len(groups[0]), *value.shape))
    return lax.all_to_all(copies, "hst", 0, 0, axis_index_groups=groups)


def broadcast_queries(slots, root):
    me = lax.axis_index("hst")
    core, x = me % CORES, me // CORES % X
    root_core, root_x, root_z = root % CORES, root // CORES % X, root // (CORES * X)
    tokens, width = slots.shape
    part = width // CORES
    own = lax.dynamic_slice_in_dim(slots, core * part, part, 1)
    other = shift(lax.dynamic_slice_in_dim(slots, (1 - core) * part, part, 1), 0, 0, 1)
    half = jnp.where(core == root_core, own, other).reshape(X, tokens // X, part)

    group = lax.dynamic_index_in_dim(half, x, 0, keepdims=False)
    for hop in range(1, X):
        sent = lax.dynamic_index_in_dim(half, (x + hop) % X, 0, keepdims=False)
        group = jnp.where((x - root_x) % X == hop, shift(sent, 0, hop, 0), group)

    columns = [[(z * X + i) * CORES + c for z in range(Z)] for i in range(X) for c in range(CORES)]
    group = lax.dynamic_index_in_dim(gather(group, columns), root_z, 0, keepdims=False)

    half = jnp.stack([group] + [shift(group, 0, hop, 0) for hop in range(1, X)])
    return jnp.stack([half, shift(half, 0, 0, 1)])


def on_device(query_slots, keys, values, counts, query_host, out_weight):
    tokens, width = query_slots.shape[1:]
    heads = width // HEAD_SIZE
    kv_heads = keys.shape[1] // HEAD_SIZE
    rows = heads // kv_heads * tokens
    groups = tokens // PIECE
    pieces = heads * groups
    root = query_host[0]

    with jax.named_scope("queries"):
        queries = broadcast_queries(query_slots[0], root)

    with jax.named_scope("attend"):
        me = lax.axis_index("hst")
        last = counts[0]
        first = jnp.where(me == root, last - tokens + 1, last)
        scalars = jnp.stack([first, last, me % CORES, me // CORES % X])
        packed = kernel_call(
            attend_kernel,
            jax.ShapeDtypeStruct((pieces, PIECE + 8, HEAD_SIZE), jnp.bfloat16),
            [SMEM, VMEM, HBM, HBM],
            [
                pltpu.VMEM((kv_heads, rows, HEAD_SIZE), jnp.bfloat16),
                pltpu.VMEM(keys.shape, jnp.bfloat16),
                pltpu.VMEM(values.shape, jnp.bfloat16),
                pltpu.VMEM((kv_heads, 1, rows), jnp.float32),
                pltpu.VMEM((kv_heads, HEAD_SIZE + 16, rows), jnp.float32),
                pltpu.SemaphoreType.DMA((2, keys.shape[0] // CHUNK)),
            ],
            vmem=60,
            name="attend",
        )(scalars, queries, keys, values)

    with jax.named_scope("merge"):
        packed = lax.all_to_all(packed, "hst", 0, 0)
        attended = kernel_call(
            merge_kernel,
            jax.ShapeDtypeStruct((pieces // CORES, PIECE, HEAD_SIZE), jnp.bfloat16),
            [VMEM],
            name="merge",
        )(packed)
        chips = [[chip * CORES + core for chip in range(Z * X)] for core in range(CORES)]
        attended = lax.all_to_all(attended, "hst", 0, 0, axis_index_groups=chips)
        sibling = shift(attended, 0, 0, 1)

    with jax.named_scope("project"):
        projected = kernel_call(
            project_kernel,
            jax.ShapeDtypeStruct((groups, PIECE, out_weight.shape[1]), jnp.float32),
            [SMEM, VMEM, VMEM, VMEM],
            name="project",
        )(scalars, attended, sibling, out_weight)
        n = lax.axis_size("tensor")
        mine = lax.axis_index("tensor")
        total = lax.dynamic_index_in_dim(projected, mine, 0, keepdims=False)
        for hop in range(1, n):
            part = lax.dynamic_index_in_dim(projected, (mine + hop) % n, 0, keepdims=False)
            total += lax.ppermute(part, "tensor", [(i, (i + hop) % n) for i in range(n)])
        return total.astype(jnp.bfloat16)


def solution(mesh):
    placed = (
        P("hst", None, "tensor"),
        P("hst", "tensor"),
        P("hst", "tensor"),
        P("hst"),
        P(),
        P("tensor", "hst"),
    )
    return jax.shard_map(
        on_device, mesh=mesh, in_specs=placed, out_specs=P("tensor", "hst"), check_vma=False
    )
```

```python
import functools

import jax
import jax.numpy as jnp
from jax import lax
from jax.experimental import pallas as pl
from jax.experimental.pallas import tpu as pltpu
from jax.sharding import PartitionSpec as P

HEAD_SIZE = 128
PIECE = 16
CHUNK = 1024
STAGES = (0, 1024, 4096)
LOG2E = 1.4426950408889634
SCORE_SCALE = LOG2E * HEAD_SIZE ** (-0.5)
MASKED = -1e30
SAMPLE = 128
SUM_LIMIT = 2.0**64
Z, X, CORES = 8, 4, 2
HBM = pl.BlockSpec(memory_space=pl.ANY)
VMEM = pl.BlockSpec(memory_space=pltpu.VMEM)
SMEM = pl.BlockSpec(memory_space=pltpu.SMEM)


def dot(lhs, rhs, lhs_dim, rhs_dim):
    return lax.dot_general(
        lhs, rhs, (((lhs_dim,), (rhs_dim,)), ((), ())), preferred_element_type=jnp.float32
    )


def attend_kernel(
    scalars_ref, own_ref, other_ref, keys_hbm, values_hbm, kept_ref, sent_ref,
    queries, keys_ref, values_ref, row_max, arrivals,
):
    rows = queries.shape[1]
    results = (kept_ref, sent_ref)
    first_limit = scalars_ref[0]
    last_limit = scalars_ref[1]
    my_core = scalars_ref[2]
    my_x = scalars_ref[3]
    chunks = pl.cdiv(last_limit, CHUNK)

    copies = []
    for stage, (start, stop) in enumerate(zip(STAGES, (*STAGES[1:], keys_hbm.shape[0]))):
        place = pl.ds(start, stop - start)
        copies.append(
            [
                pltpu.make_async_copy(source.at[place], target.at[place], arrivals.at[kind, stage])
                for kind, (source, target) in enumerate(
                    ((keys_hbm, keys_ref), (values_hbm, values_ref))
                )
            ]
        )
        for copy in copies[-1]:
            copy.start()

    def await_stage(stage):
        for copy in copies[stage]:
            copy.wait()

    def column_of(head):
        column = my_core if head == 0 else 1 - my_core
        return pl.ds(pl.multiple_of(column * HEAD_SIZE, HEAD_SIZE), HEAD_SIZE)

    def loop(start, stop, body):
        def one(chunk, carry):
            body(chunk)
            return carry

        lax.fori_loop(start, stop, one, 0)

    for head, source in enumerate((own_ref, other_ref)):
        groups, _, columns = source.shape
        tokens = groups * PIECE
        for group in range(groups):
            piece = source[lax.rem(my_x - group + groups, groups)]
            for part in range(columns // HEAD_SIZE):
                queries[head, pl.ds((part * groups + group) * PIECE, PIECE)] = piece[
                    :, part * HEAD_SIZE : (part + 1) * HEAD_SIZE
                ]

    def step(chunk, masked, running, first=False):
        base = pl.multiple_of(chunk * CHUNK, CHUNK)
        place = pl.ds(base, CHUNK)
        for head, result in enumerate(results):
            scores = dot(keys_ref[place, column_of(head)], queries[head], 1, 1) * SCORE_SCALE
            if masked:
                token = lax.rem(lax.broadcasted_iota(jnp.int32, (1, rows), 1), tokens)
                limit = jnp.minimum(first_limit + token, last_limit)
                slot = lax.broadcasted_iota(jnp.int32, scores.shape, 0) + base
                scores = jnp.where(slot < limit, scores, MASKED)
            if first:
                row_max[head] = jnp.max(scores[:SAMPLE], axis=0, keepdims=True)
            if running:
                before = row_max[head]
                row_max[head] = jnp.maximum(before, jnp.max(scores, axis=0, keepdims=True))
                result[...] *= jnp.exp2(before - row_max[head])
            weights = jnp.exp2(scores - row_max[head]).astype(jnp.bfloat16)
            values = values_ref[place, column_of(head)]
            lhs = jnp.concatenate([values.T, jnp.ones((16, CHUNK), jnp.bfloat16)], axis=0)
            part = dot(lhs, weights, 1, 0)
            result[...] = part if first else result[...] + part

    def arrived_step(chunk, masked):
        for stage, start in enumerate(STAGES[1:], 1):
            pl.when(chunk == start // CHUNK)(functools.partial(await_stage, stage))
        step(chunk, masked, False)

    whole = first_limit // CHUNK
    await_stage(0)
    step(0, False, False, True)
    loop(1, whole, lambda chunk: arrived_step(chunk, False))
    loop(whole, chunks, lambda chunk: arrived_step(chunk, True))
    for stage, start in enumerate(STAGES[1:], 1):
        pl.when(chunks <= start // CHUNK)(functools.partial(await_stage, stage))

    over = jnp.zeros((1, rows), jnp.int32)
    for result in results:
        over += jnp.where(result[HEAD_SIZE : HEAD_SIZE + 1] < SUM_LIMIT, 0, 1)

    @pl.when(jnp.sum(over) > 0)
    def _():
        row_max[...] = jnp.full_like(row_max, MASKED)
        for result in results:
            result[...] = jnp.zeros_like(result)
        loop(0, chunks, lambda chunk: step(chunk, True, True))

    for head, result in enumerate(results):
        result[HEAD_SIZE + 8 :] = jnp.broadcast_to(row_max[head], (8, rows))


def pair_kernel(kept_ref, received_ref, packed_ref):
    rows = kept_ref.shape[1]
    pieces = rows // PIECE
    total_row = slice(HEAD_SIZE, HEAD_SIZE + 1)
    max_row = slice(HEAD_SIZE + 8, HEAD_SIZE + 9)
    peak = jnp.maximum(kept_ref[max_row], received_ref[max_row])
    peak = peak.astype(jnp.bfloat16).astype(jnp.float32)
    kept_factor = jnp.exp2(kept_ref[max_row] - peak)
    received_factor = jnp.exp2(received_ref[max_row] - peak)
    total = kept_ref[total_row] * kept_factor + received_ref[total_row] * received_factor
    out = (
        kept_ref[:HEAD_SIZE] * (kept_factor / total)
        + received_ref[:HEAD_SIZE] * (received_factor / total)
    ).T.astype(jnp.bfloat16)
    high = total.astype(jnp.bfloat16).astype(jnp.float32)
    row = lax.broadcasted_iota(jnp.int32, (pieces, PIECE, HEAD_SIZE), 1)
    lane = lax.broadcasted_iota(jnp.int32, (pieces, PIECE, HEAD_SIZE), 2)

    def spread(value):
        return jnp.broadcast_to(value, (HEAD_SIZE, rows)).T.reshape(pieces, PIECE, HEAD_SIZE)

    stats = jnp.where(lane == row, spread(peak), 0.0)
    stats = jnp.where(lane == row + PIECE, spread(high), stats)
    stats = jnp.where(lane == row + 2 * PIECE, spread(total - high), stats)
    stats = jnp.sum(stats, axis=1, keepdims=True).astype(jnp.bfloat16)
    packed_ref[:, :PIECE] = out.reshape(pieces, PIECE, HEAD_SIZE)
    packed_ref[:, PIECE:] = jnp.broadcast_to(stats, (pieces, 8, HEAD_SIZE))


def merge_kernel(packed_ref, attended_ref):
    chips = packed_ref.shape[0]
    stats = jnp.max(packed_ref[:, PIECE:].astype(jnp.float32), axis=1).T
    row_max = stats[:PIECE]
    totals = stats[PIECE : 2 * PIECE] + stats[2 * PIECE : 3 * PIECE]
    peak = jnp.max(row_max, axis=1, keepdims=True)
    shares = totals * jnp.exp2(row_max - peak)
    shares = shares / jnp.sum(shares, axis=1, keepdims=True)
    merged = jnp.zeros(attended_ref.shape, jnp.float32)
    for chip in range(chips):
        merged += shares[:, chip : chip + 1] * packed_ref[chip, :PIECE].astype(jnp.float32)
    attended_ref[...] = merged.astype(jnp.bfloat16)


def project_kernel(scalars_ref, own_ref, sibling_ref, *refs):
    *weight_refs, out_ref = refs
    shares = len(weight_refs)
    my_core, my_share = scalars_ref[2], scalars_ref[4]
    heads = own_ref.shape[0] // shares
    depth = heads * HEAD_SIZE
    total = jnp.zeros(out_ref.shape, jnp.float32)
    for slot, weight_ref in enumerate(weight_refs):
        share = lax.rem(my_share - slot + shares, shares)
        for source, core in ((own_ref, my_core), (sibling_ref, 1 - my_core)):
            lhs = jnp.concatenate([source[head * shares + share] for head in range(heads)], axis=1)
            total += dot(lhs, weight_ref[pl.ds(pl.multiple_of(core * depth, depth), depth)], 1, 0)
    out_ref[...] = total.astype(out_ref.dtype)


def kernel_call(body, out_shape, in_specs, scratch=(), vmem=40, name=None):
    return pl.pallas_call(
        body,
        out_shape=out_shape,
        in_specs=in_specs,
        out_specs=jax.tree.map(lambda _: VMEM, out_shape),
        scratch_shapes=scratch,
        compiler_params=pltpu.CompilerParams(vmem_limit_bytes=vmem << 20),
        name=name,
    )


def shift(value, dz, dx, dcore):
    def index(z, x, core):
        return ((z % Z) * X + x % X) * CORES + core % CORES

    pairs = [
        (index(z, x, core), index(z + dz, x + dx, core + dcore))
        for z in range(Z)
        for x in range(X)
        for core in range(CORES)
    ]
    return lax.ppermute(value, "hst", pairs)


def gather(value, groups):
    copies = jnp.broadcast_to(value[None], (len(groups[0]), *value.shape))
    return lax.all_to_all(copies, "hst", 0, 0, axis_index_groups=groups)


def broadcast_queries(slots, root):
    me = lax.axis_index("hst")
    core, x = me % CORES, me // CORES % X
    root_core, root_x, root_z = root % CORES, root // CORES % X, root // (CORES * X)
    tokens, width = slots.shape
    part = width // CORES
    served = jnp.where(core == root_core, slots, shift(slots, 0, 0, 1))
    half = lax.dynamic_slice_in_dim(served, core * part, part, 1).reshape(X, tokens // X, part)

    group = lax.dynamic_index_in_dim(half, x, 0, keepdims=False)
    for hop in range(1, X):
        sent = lax.dynamic_index_in_dim(half, (x + hop) % X, 0, keepdims=False)
        group = jnp.where((x - root_x) % X == hop, shift(sent, 0, hop, 0), group)

    columns = [[(z * X + i) * CORES + c for z in range(Z)] for i in range(X) for c in range(CORES)]
    group = lax.dynamic_index_in_dim(gather(group, columns), root_z, 0, keepdims=False)

    half = jnp.stack([group] + [shift(group, 0, hop, 0) for hop in range(1, X)])
    return half, shift(half, 0, 0, 1)


def to_token_groups(piece, share_count, piece_count):
    pairs = []
    for share in range(share_count):
        for place in range(piece_count):
            head, group = divmod(place, share_count)
            for core in range(CORES):
                source = (place * CORES + core) * share_count + share
                target = ((head * share_count + share) * CORES + core) * share_count + group
                pairs.append((source, target))
    return lax.ppermute(piece, ("hst", "tensor"), pairs)


def on_device(query_slots, keys, values, counts, query_host, out_weight):
    tokens, width = query_slots.shape[1:]
    kv_heads = keys.shape[1] // HEAD_SIZE
    rows = width // keys.shape[1] * tokens
    pieces = rows // PIECE
    root = query_host[0]
    me = lax.axis_index("hst")
    share = lax.axis_index("tensor")
    shares = lax.axis_size("tensor")

    weights = [out_weight] + [
        lax.ppermute(out_weight, "tensor", [(i, (i + hop) % shares) for i in range(shares)])
        for hop in range(1, shares)
    ]

    with jax.named_scope("queries"):
        own, other = broadcast_queries(query_slots[0], root)
        own, other, weights = lax.optimization_barrier((own, other, weights))

    with jax.named_scope("attend"):
        last = counts[0]
        first = jnp.where(me == root, last - tokens + 1, last)
        scalars = jnp.stack([first, last, me % CORES, me // CORES % X, share])
        result = jax.ShapeDtypeStruct((HEAD_SIZE + 16, rows), jnp.float32)
        kept, sent = kernel_call(
            attend_kernel,
            (result, result),
            [SMEM, VMEM, VMEM, HBM, HBM],
            [
                pltpu.VMEM((kv_heads, rows, HEAD_SIZE), jnp.bfloat16),
                pltpu.VMEM(keys.shape, jnp.bfloat16),
                pltpu.VMEM(values.shape, jnp.bfloat16),
                pltpu.VMEM((kv_heads, 1, rows), jnp.float32),
                pltpu.SemaphoreType.DMA((2, len(STAGES))),
            ],
            vmem=51,
            name="attend",
        )(scalars, own, other, keys, values)

    with jax.named_scope("merge"):
        packed = kernel_call(
            pair_kernel,
            jax.ShapeDtypeStruct((pieces, PIECE + 8, HEAD_SIZE), jnp.bfloat16),
            [VMEM, VMEM],
            name="pair",
        )(kept, shift(sent, 0, 0, 1))
        chips = [[chip * CORES + core for chip in range(Z * X)] for core in range(CORES)]
        packed = lax.all_to_all(packed, "hst", 0, 0, axis_index_groups=chips)
        attended = kernel_call(
            merge_kernel,
            jax.ShapeDtypeStruct((PIECE, HEAD_SIZE), jnp.bfloat16),
            [VMEM],
            name="merge",
        )(packed)

    with jax.named_scope("project"):
        attended = gather(to_token_groups(attended, shares, pieces), chips)
        return kernel_call(
            project_kernel,
            jax.ShapeDtypeStruct((PIECE, out_weight.shape[1]), jnp.bfloat16),
            [SMEM] + [VMEM] * (2 + shares),
            name="project",
        )(scalars, attended, shift(attended, 0, 0, 1), *weights)


def solution(mesh):
    placed = (
        P("hst", None, "tensor"),
        P("hst", "tensor"),
        P("hst", "tensor"),
        P("hst"),
        P(),
        P("tensor", "hst"),
    )
    return jax.shard_map(
        on_device, mesh=mesh, in_specs=placed, out_specs=P("tensor", "hst"), check_vma=False
    )
```

```python
import functools

import jax
import jax.numpy as jnp
from jax import lax
from jax.experimental import pallas as pl
from jax.experimental.pallas import tpu as pltpu
from jax.sharding import PartitionSpec as P

HEAD_SIZE = 128
PIECE = 16
CHUNK = 1024
STAGES = (0, 1024, 4096)
LOG2E = 1.4426950408889634
SCORE_SCALE = LOG2E * HEAD_SIZE ** (-0.5)
MASKED = -1e30
SAMPLE = 128
SUM_LIMIT = 2.0**64
Z, X, CORES = 8, 4, 2
HBM = pl.BlockSpec(memory_space=pl.ANY)
VMEM = pl.BlockSpec(memory_space=pltpu.VMEM)
SMEM = pl.BlockSpec(memory_space=pltpu.SMEM)


def dot(lhs, rhs, lhs_dim, rhs_dim):
    return lax.dot_general(
        lhs, rhs, (((lhs_dim,), (rhs_dim,)), ((), ())), preferred_element_type=jnp.float32
    )


def attend_kernel(
    scalars_ref, own_ref, other_ref, keys_hbm, values_hbm, kept_ref, sent_ref,
    queries, keys_ref, values_ref, row_max, arrivals,
):
    rows = queries.shape[1]
    results = (kept_ref, sent_ref)
    first_limit = scalars_ref[0]
    last_limit = scalars_ref[1]
    my_core = scalars_ref[2]
    my_x = scalars_ref[3]
    chunks = pl.cdiv(last_limit, CHUNK)

    copies = []
    for stage, (start, stop) in enumerate(zip(STAGES, (*STAGES[1:], keys_hbm.shape[0]))):
        place = pl.ds(start, stop - start)
        copies.append(
            [
                pltpu.make_async_copy(source.at[place], target.at[place], arrivals.at[kind, stage])
                for kind, (source, target) in enumerate(
                    ((keys_hbm, keys_ref), (values_hbm, values_ref))
                )
            ]
        )
        for copy in copies[-1]:
            copy.start()

    def await_stage(stage):
        for copy in copies[stage]:
            copy.wait()

    def column_of(head):
        column = my_core if head == 0 else 1 - my_core
        return pl.ds(pl.multiple_of(column * HEAD_SIZE, HEAD_SIZE), HEAD_SIZE)

    def loop(start, stop, body):
        def one(chunk, carry):
            body(chunk)
            return carry

        lax.fori_loop(start, stop, one, 0)

    for head, source in enumerate((own_ref, other_ref)):
        groups, _, columns = source.shape
        tokens = groups * PIECE
        for group in range(groups):
            piece = source[lax.rem(my_x - group + groups, groups)]
            for part in range(columns // HEAD_SIZE):
                queries[head, pl.ds((part * groups + group) * PIECE, PIECE)] = piece[
                    :, part * HEAD_SIZE : (part + 1) * HEAD_SIZE
                ]

    def step(chunk, masked, running, first=False):
        base = pl.multiple_of(chunk * CHUNK, CHUNK)
        place = pl.ds(base, CHUNK)
        for head, result in enumerate(results):
            scores = dot(keys_ref[place, column_of(head)], queries[head], 1, 1) * SCORE_SCALE
            if masked:
                token = lax.rem(lax.broadcasted_iota(jnp.int32, (1, rows), 1), tokens)
                limit = jnp.minimum(first_limit + token, last_limit)
                slot = lax.broadcasted_iota(jnp.int32, scores.shape, 0) + base
                scores = jnp.where(slot < limit, scores, MASKED)
            if first:
                row_max[head] = jnp.max(scores[:SAMPLE], axis=0, keepdims=True)
            if running:
                before = row_max[head]
                row_max[head] = jnp.maximum(before, jnp.max(scores, axis=0, keepdims=True))
                result[...] *= jnp.exp2(before - row_max[head])
            weights = jnp.exp2(scores - row_max[head]).astype(jnp.bfloat16)
            values = values_ref[place, column_of(head)]
            lhs = jnp.concatenate([values.T, jnp.ones((16, CHUNK), jnp.bfloat16)], axis=0)
            part = dot(lhs, weights, 1, 0)
            result[...] = part if first else result[...] + part

    def arrived_step(chunk, masked):
        for stage, start in enumerate(STAGES[1:], 1):
            pl.when(chunk == start // CHUNK)(functools.partial(await_stage, stage))
        step(chunk, masked, False)

    whole = first_limit // CHUNK
    await_stage(0)
    step(0, False, False, True)
    loop(1, whole, lambda chunk: arrived_step(chunk, False))
    loop(whole, chunks, lambda chunk: arrived_step(chunk, True))
    for stage, start in enumerate(STAGES[1:], 1):
        pl.when(chunks <= start // CHUNK)(functools.partial(await_stage, stage))

    over = jnp.zeros((1, rows), jnp.int32)
    for result in results:
        over += jnp.where(result[HEAD_SIZE : HEAD_SIZE + 1] < SUM_LIMIT, 0, 1)

    @pl.when(jnp.sum(over) > 0)
    def _():
        row_max[...] = jnp.full_like(row_max, MASKED)
        for result in results:
            result[...] = jnp.zeros_like(result)
        loop(0, chunks, lambda chunk: step(chunk, True, True))

    for head, result in enumerate(results):
        result[HEAD_SIZE + 8 :] = jnp.broadcast_to(row_max[head], (8, rows))


def pair_kernel(kept_ref, received_ref, packed_ref):
    rows = kept_ref.shape[1]
    pieces = rows // PIECE
    total_row = slice(HEAD_SIZE, HEAD_SIZE + 1)
    max_row = slice(HEAD_SIZE + 8, HEAD_SIZE + 9)
    peak = jnp.maximum(kept_ref[max_row], received_ref[max_row])
    peak = peak.astype(jnp.bfloat16).astype(jnp.float32)
    kept_factor = jnp.exp2(kept_ref[max_row] - peak)
    received_factor = jnp.exp2(received_ref[max_row] - peak)
    total = kept_ref[total_row] * kept_factor + received_ref[total_row] * received_factor
    out = (
        kept_ref[:HEAD_SIZE] * (kept_factor / total)
        + received_ref[:HEAD_SIZE] * (received_factor / total)
    ).T.astype(jnp.bfloat16)
    high = total.astype(jnp.bfloat16).astype(jnp.float32)
    row = lax.broadcasted_iota(jnp.int32, (pieces, PIECE, HEAD_SIZE), 1)
    lane = lax.broadcasted_iota(jnp.int32, (pieces, PIECE, HEAD_SIZE), 2)

    def spread(value):
        return jnp.broadcast_to(value, (HEAD_SIZE, rows)).T.reshape(pieces, PIECE, HEAD_SIZE)

    stats = jnp.where(lane == row, spread(peak), 0.0)
    stats = jnp.where(lane == row + PIECE, spread(high), stats)
    stats = jnp.where(lane == row + 2 * PIECE, spread(total - high), stats)
    stats = jnp.sum(stats, axis=1, keepdims=True).astype(jnp.bfloat16)
    packed_ref[:, :PIECE] = out.reshape(pieces, PIECE, HEAD_SIZE)
    packed_ref[:, PIECE:] = jnp.broadcast_to(stats, (pieces, 8, HEAD_SIZE))


def merge_kernel(packed_ref, attended_ref):
    chips = packed_ref.shape[0]
    stats = jnp.max(packed_ref[:, PIECE:].astype(jnp.float32), axis=1).T
    row_max = stats[:PIECE]
    totals = stats[PIECE : 2 * PIECE] + stats[2 * PIECE : 3 * PIECE]
    peak = jnp.max(row_max, axis=1, keepdims=True)
    shares = totals * jnp.exp2(row_max - peak)
    shares = shares / jnp.sum(shares, axis=1, keepdims=True)
    merged = jnp.zeros(attended_ref.shape[1:], jnp.float32)
    for chip in range(chips):
        merged += shares[:, chip : chip + 1] * packed_ref[chip, :PIECE].astype(jnp.float32)
    attended_ref[...] = jnp.broadcast_to(merged.astype(jnp.bfloat16)[None], attended_ref.shape)


def project_kernel(scalars_ref, own_ref, sibling_ref, weight_ref, out_ref):
    my_core = scalars_ref[2]
    groups = out_ref.shape[0]
    heads = own_ref.shape[0] // groups
    depth = heads * HEAD_SIZE
    total = jnp.zeros((groups * PIECE, out_ref.shape[2]), jnp.float32)
    for source, core in ((own_ref, my_core), (sibling_ref, 1 - my_core)):
        lhs = jnp.concatenate(
            [
                source[head * groups : (head + 1) * groups].reshape(-1, HEAD_SIZE)
                for head in range(heads)
            ],
            axis=1,
        )
        total += dot(lhs, weight_ref[pl.ds(pl.multiple_of(core * depth, depth), depth)], 1, 0)
    out_ref[...] = total.reshape(out_ref.shape)


def kernel_call(body, out_shape, in_specs, scratch=(), vmem=40, name=None):
    return pl.pallas_call(
        body,
        out_shape=out_shape,
        in_specs=in_specs,
        out_specs=jax.tree.map(lambda _: VMEM, out_shape),
        scratch_shapes=scratch,
        compiler_params=pltpu.CompilerParams(vmem_limit_bytes=vmem << 20),
        name=name,
    )


def shift(value, dz, dx, dcore):
    def index(z, x, core):
        return ((z % Z) * X + x % X) * CORES + core % CORES

    pairs = [
        (index(z, x, core), index(z + dz, x + dx, core + dcore))
        for z in range(Z)
        for x in range(X)
        for core in range(CORES)
    ]
    return lax.ppermute(value, "hst", pairs)


def gather(value, groups):
    copies = jnp.broadcast_to(value[None], (len(groups[0]), *value.shape))
    return lax.all_to_all(copies, "hst", 0, 0, axis_index_groups=groups)


def broadcast_queries(slots, root):
    me = lax.axis_index("hst")
    core, x = me % CORES, me // CORES % X
    root_core, root_x, root_z = root % CORES, root // CORES % X, root // (CORES * X)
    tokens, width = slots.shape
    part = width // CORES
    served = jnp.where(core == root_core, slots, shift(slots, 0, 0, 1))
    half = lax.dynamic_slice_in_dim(served, core * part, part, 1).reshape(X, tokens // X, part)

    group = lax.dynamic_index_in_dim(half, x, 0, keepdims=False)
    for hop in range(1, X):
        sent = lax.dynamic_index_in_dim(half, (x + hop) % X, 0, keepdims=False)
        group = jnp.where((x - root_x) % X == hop, shift(sent, 0, hop, 0), group)

    columns = [[(z * X + i) * CORES + c for z in range(Z)] for i in range(X) for c in range(CORES)]
    group = lax.dynamic_index_in_dim(gather(group, columns), root_z, 0, keepdims=False)

    half = jnp.stack([group] + [shift(group, 0, hop, 0) for hop in range(1, X)])
    return half, shift(half, 0, 0, 1)


def on_device(query_slots, keys, values, counts, query_host, out_weight):
    tokens, width = query_slots.shape[1:]
    kv_heads = keys.shape[1] // HEAD_SIZE
    rows = width // keys.shape[1] * tokens
    pieces = rows // PIECE
    root = query_host[0]
    me = lax.axis_index("hst")

    with jax.named_scope("queries"):
        own, other = broadcast_queries(query_slots[0], root)

    with jax.named_scope("attend"):
        last = counts[0]
        first = jnp.where(me == root, last - tokens + 1, last)
        scalars = jnp.stack([first, last, me % CORES, me // CORES % X])
        result = jax.ShapeDtypeStruct((HEAD_SIZE + 16, rows), jnp.float32)
        kept, sent = kernel_call(
            attend_kernel,
            (result, result),
            [SMEM, VMEM, VMEM, HBM, HBM],
            [
                pltpu.VMEM((kv_heads, rows, HEAD_SIZE), jnp.bfloat16),
                pltpu.VMEM(keys.shape, jnp.bfloat16),
                pltpu.VMEM(values.shape, jnp.bfloat16),
                pltpu.VMEM((kv_heads, 1, rows), jnp.float32),
                pltpu.SemaphoreType.DMA((2, len(STAGES))),
            ],
            vmem=51,
            name="attend",
        )(scalars, own, other, keys, values)

    with jax.named_scope("merge"):
        packed = kernel_call(
            pair_kernel,
            jax.ShapeDtypeStruct((pieces, PIECE + 8, HEAD_SIZE), jnp.bfloat16),
            [VMEM, VMEM],
            name="pair",
        )(kept, shift(sent, 0, 0, 1))
        chips = [[chip * CORES + core for chip in range(Z * X)] for core in range(CORES)]
        packed = lax.all_to_all(packed, "hst", 0, 0, axis_index_groups=chips)
        attended = kernel_call(
            merge_kernel,
            jax.ShapeDtypeStruct((pieces, PIECE, HEAD_SIZE), jnp.bfloat16),
            [VMEM],
            name="merge",
        )(packed)
        attended = lax.all_to_all(attended, "hst", 0, 0, axis_index_groups=chips)

    with jax.named_scope("project"):
        projected = kernel_call(
            project_kernel,
            jax.ShapeDtypeStruct((tokens // PIECE, PIECE, out_weight.shape[1]), jnp.float32),
            [SMEM] + [VMEM] * 3,
            name="project",
        )(scalars, attended, shift(attended, 0, 0, 1), out_weight)
        shares = lax.axis_size("tensor")
        mine = lax.axis_index("tensor")
        total = lax.dynamic_index_in_dim(projected, mine, 0, keepdims=False)
        for hop in range(1, shares):
            part = lax.dynamic_index_in_dim(projected, (mine + hop) % shares, 0, keepdims=False)
            total += lax.ppermute(part, "tensor", [(i, (i + hop) % shares) for i in range(shares)])
        return total.astype(jnp.bfloat16)


def solution(mesh):
    placed = (
        P("hst", None, "tensor"),
        P("hst", "tensor"),
        P("hst", "tensor"),
        P("hst"),
        P(),
        P("tensor", "hst"),
    )
    return jax.shard_map(
        on_device, mesh=mesh, in_specs=placed, out_specs=P("tensor", "hst"), check_vma=False
    )
```

```python
import functools

import jax
import jax.numpy as jnp
from jax import lax
from jax.experimental import pallas as pl
from jax.experimental.pallas import tpu as pltpu
from jax.sharding import PartitionSpec as P

HEAD_SIZE = 128
PIECE = 16
CHUNK = 1024
STAGES = (0, 1024, 4096)
LOG2E = 1.4426950408889634
SCORE_SCALE = LOG2E * HEAD_SIZE ** (-0.5)
MASKED = -1e30
SAMPLE = 128
SUM_LIMIT = 2.0**64
Z, X, CORES = 8, 4, 2
HBM = pl.BlockSpec(memory_space=pl.ANY)
VMEM = pl.BlockSpec(memory_space=pltpu.VMEM)
SMEM = pl.BlockSpec(memory_space=pltpu.SMEM)


def dot(lhs, rhs, lhs_dim, rhs_dim):
    return lax.dot_general(
        lhs, rhs, (((lhs_dim,), (rhs_dim,)), ((), ())), preferred_element_type=jnp.float32
    )


def attend_kernel(
    scalars_ref, own_ref, other_ref, keys_hbm, values_hbm, kept_ref, sent_ref,
    queries, keys_ref, values_ref, row_max, arrivals,
):
    rows = queries.shape[1]
    results = (kept_ref, sent_ref)
    first_limit = scalars_ref[0]
    last_limit = scalars_ref[1]
    my_core = scalars_ref[2]
    my_x = scalars_ref[3]
    chunks = pl.cdiv(last_limit, CHUNK)

    copies = []
    for stage, (start, stop) in enumerate(zip(STAGES, (*STAGES[1:], keys_hbm.shape[0]))):
        place = pl.ds(start, stop - start)
        copies.append(
            [
                pltpu.make_async_copy(source.at[place], target.at[place], arrivals.at[kind, stage])
                for kind, (source, target) in enumerate(
                    ((keys_hbm, keys_ref), (values_hbm, values_ref))
                )
            ]
        )
        for copy in copies[-1]:
            copy.start()

    def await_stage(stage):
        for copy in copies[stage]:
            copy.wait()

    def column_of(head):
        column = my_core if head == 0 else 1 - my_core
        return pl.ds(pl.multiple_of(column * HEAD_SIZE, HEAD_SIZE), HEAD_SIZE)

    def loop(start, stop, body):
        def one(chunk, carry):
            body(chunk)
            return carry

        lax.fori_loop(start, stop, one, 0)

    for head, source in enumerate((own_ref, other_ref)):
        groups, _, columns = source.shape
        tokens = groups * PIECE
        for group in range(groups):
            piece = source[lax.rem(my_x - group + groups, groups)]
            for part in range(columns // HEAD_SIZE):
                queries[head, pl.ds((part * groups + group) * PIECE, PIECE)] = piece[
                    :, part * HEAD_SIZE : (part + 1) * HEAD_SIZE
                ]

    def step(chunk, masked, running, first=False):
        base = pl.multiple_of(chunk * CHUNK, CHUNK)
        place = pl.ds(base, CHUNK)
        for head, result in enumerate(results):
            scores = dot(keys_ref[place, column_of(head)], queries[head], 1, 1) * SCORE_SCALE
            if masked:
                token = lax.rem(lax.broadcasted_iota(jnp.int32, (1, rows), 1), tokens)
                limit = jnp.minimum(first_limit + token, last_limit)
                slot = lax.broadcasted_iota(jnp.int32, scores.shape, 0) + base
                scores = jnp.where(slot < limit, scores, MASKED)
            if first:
                row_max[head] = jnp.max(scores[:SAMPLE], axis=0, keepdims=True)
            if running:
                before = row_max[head]
                row_max[head] = jnp.maximum(before, jnp.max(scores, axis=0, keepdims=True))
                result[...] *= jnp.exp2(before - row_max[head])
            weights = jnp.exp2(scores - row_max[head]).astype(jnp.bfloat16)
            values = values_ref[place, column_of(head)]
            lhs = jnp.concatenate([values.T, jnp.ones((16, CHUNK), jnp.bfloat16)], axis=0)
            part = dot(lhs, weights, 1, 0)
            result[...] = part if first else result[...] + part

    def arrived_step(chunk, masked):
        for stage, start in enumerate(STAGES[1:], 1):
            pl.when(chunk == start // CHUNK)(functools.partial(await_stage, stage))
        step(chunk, masked, False)

    whole = first_limit // CHUNK
    await_stage(0)
    step(0, False, False, True)
    loop(1, whole, lambda chunk: arrived_step(chunk, False))
    loop(whole, chunks, lambda chunk: arrived_step(chunk, True))
    for stage, start in enumerate(STAGES[1:], 1):
        pl.when(chunks <= start // CHUNK)(functools.partial(await_stage, stage))

    over = jnp.zeros((1, rows), jnp.int32)
    for result in results:
        over += jnp.where(result[HEAD_SIZE : HEAD_SIZE + 1] < SUM_LIMIT, 0, 1)

    @pl.when(jnp.sum(over) > 0)
    def _():
        row_max[...] = jnp.full_like(row_max, MASKED)
        for result in results:
            result[...] = jnp.zeros_like(result)
        loop(0, chunks, lambda chunk: step(chunk, True, True))

    for head, result in enumerate(results):
        result[HEAD_SIZE + 8 :] = jnp.broadcast_to(row_max[head], (8, rows))


def pair_kernel(kept_ref, received_ref, packed_ref):
    rows = kept_ref.shape[1]
    pieces = rows // PIECE
    total_row = slice(HEAD_SIZE, HEAD_SIZE + 1)
    max_row = slice(HEAD_SIZE + 8, HEAD_SIZE + 9)
    peak = jnp.maximum(kept_ref[max_row], received_ref[max_row])
    peak = peak.astype(jnp.bfloat16).astype(jnp.float32)
    kept_factor = jnp.exp2(kept_ref[max_row] - peak)
    received_factor = jnp.exp2(received_ref[max_row] - peak)
    total = kept_ref[total_row] * kept_factor + received_ref[total_row] * received_factor
    out = (
        kept_ref[:HEAD_SIZE] * (kept_factor / total)
        + received_ref[:HEAD_SIZE] * (received_factor / total)
    ).T.astype(jnp.bfloat16)
    high = total.astype(jnp.bfloat16).astype(jnp.float32)
    row = lax.broadcasted_iota(jnp.int32, (pieces, PIECE, HEAD_SIZE), 1)
    lane = lax.broadcasted_iota(jnp.int32, (pieces, PIECE, HEAD_SIZE), 2)

    def spread(value):
        return jnp.broadcast_to(value, (HEAD_SIZE, rows)).T.reshape(pieces, PIECE, HEAD_SIZE)

    stats = jnp.where(lane == row, spread(peak), 0.0)
    stats = jnp.where(lane == row + PIECE, spread(high), stats)
    stats = jnp.where(lane == row + 2 * PIECE, spread(total - high), stats)
    stats = jnp.sum(stats, axis=1, keepdims=True).astype(jnp.bfloat16)
    packed_ref[:, :PIECE] = out.reshape(pieces, PIECE, HEAD_SIZE)
    packed_ref[:, PIECE:] = jnp.broadcast_to(stats, (pieces, 8, HEAD_SIZE))


def merge_kernel(packed_ref, attended_ref):
    chips = packed_ref.shape[0]
    stats = jnp.max(packed_ref[:, PIECE:].astype(jnp.float32), axis=1).T
    row_max = stats[:PIECE]
    totals = stats[PIECE : 2 * PIECE] + stats[2 * PIECE : 3 * PIECE]
    peak = jnp.max(row_max, axis=1, keepdims=True)
    shares = totals * jnp.exp2(row_max - peak)
    shares = shares / jnp.sum(shares, axis=1, keepdims=True)
    merged = jnp.zeros(attended_ref.shape[1:], jnp.float32)
    for chip in range(chips):
        merged += shares[:, chip : chip + 1] * packed_ref[chip, :PIECE].astype(jnp.float32)
    attended_ref[...] = jnp.broadcast_to(merged.astype(jnp.bfloat16)[None], attended_ref.shape)


def project_kernel(scalars_ref, own_ref, sibling_ref, weight_ref, out_ref):
    my_core = scalars_ref[2]
    groups = out_ref.shape[0]
    heads = own_ref.shape[0] // groups
    depth = heads * HEAD_SIZE
    total = jnp.zeros((groups * PIECE, out_ref.shape[2]), jnp.float32)
    for source, core in ((own_ref, my_core), (sibling_ref, 1 - my_core)):
        lhs = jnp.concatenate(
            [
                source[head * groups : (head + 1) * groups].reshape(-1, HEAD_SIZE)
                for head in range(heads)
            ],
            axis=1,
        )
        total += dot(lhs, weight_ref[pl.ds(pl.multiple_of(core * depth, depth), depth)], 1, 0)
    out_ref[...] = total.reshape(out_ref.shape)


def kernel_call(body, out_shape, in_specs, scratch=(), vmem=40, name=None):
    return pl.pallas_call(
        body,
        out_shape=out_shape,
        in_specs=in_specs,
        out_specs=jax.tree.map(lambda _: VMEM, out_shape),
        scratch_shapes=scratch,
        compiler_params=pltpu.CompilerParams(vmem_limit_bytes=vmem << 20),
        name=name,
    )


def host_index(z, x, core):
    return ((z % Z) * X + x % X) * CORES + core % CORES


def shift(value, dz, dx, dcore, rows=range(Z)):
    pairs = [
        (host_index(z, x, core), host_index(z + dz, x + dx, core + dcore))
        for z in rows
        for x in range(X)
        for core in range(CORES)
    ]
    return lax.ppermute(value, "hst", pairs)


def spread_from(root_z, half, x, z, root_x):
    first = root_z // (Z // 2) * (Z // 2)
    group = lax.dynamic_index_in_dim(half, x, 0, keepdims=False)
    for hop in range(1, X):
        sent = lax.dynamic_index_in_dim(half, (x + hop) % X, 0, keepdims=False)
        received = shift(sent, 0, hop, 0, range(first, first + Z // 2))
        group = jnp.where((x - root_x) % X == hop, received, group)
    up, down = shift(group, 3, 0, 0, [root_z]), shift(group, -3, 0, 0, [root_z])
    return jnp.where(z == (root_z + 3) % Z, up, jnp.where(z == (root_z - 3) % Z, down, group))


def broadcast_queries(slots, root):
    me = lax.axis_index("hst")
    core, x, z = me % CORES, me // CORES % X, me // (CORES * X)
    root_core, root_x, root_z = root % CORES, root // CORES % X, root // (CORES * X)
    tokens, width = slots.shape
    part = width // CORES
    served = jnp.where(core == root_core, slots, shift(slots, 0, 0, 1))
    half = lax.dynamic_slice_in_dim(served, core * part, part, 1).reshape(X, tokens // X, part)

    group = lax.switch(
        root_z, [functools.partial(spread_from, row) for row in range(Z)], half, x, z, root_x
    )
    distance = (z - root_z) % Z
    up, down = shift(group, 1, 0, 0), shift(group, -1, 0, 0)
    from_below = (distance == 1) | (distance == 4) | (distance == 6)
    from_above = (distance == 2) | (distance == 7)
    group = jnp.where(from_below, up, jnp.where(from_above, down, group))

    half = jnp.stack([group] + [shift(group, 0, hop, 0) for hop in range(1, X)])
    return half, shift(half, 0, 0, 1)


def on_device(query_slots, keys, values, counts, query_host, out_weight):
    tokens, width = query_slots.shape[1:]
    kv_heads = keys.shape[1] // HEAD_SIZE
    rows = width // keys.shape[1] * tokens
    pieces = rows // PIECE
    root = query_host[0]
    me = lax.axis_index("hst")

    with jax.named_scope("queries"):
        own, other = broadcast_queries(query_slots[0], root)

    with jax.named_scope("attend"):
        last = counts[0]
        first = jnp.where(me == root, last - tokens + 1, last)
        scalars = jnp.stack([first, last, me % CORES, me // CORES % X])
        result = jax.ShapeDtypeStruct((HEAD_SIZE + 16, rows), jnp.float32)
        kept, sent = kernel_call(
            attend_kernel,
            (result, result),
            [SMEM, VMEM, VMEM, HBM, HBM],
            [
                pltpu.VMEM((kv_heads, rows, HEAD_SIZE), jnp.bfloat16),
                pltpu.VMEM(keys.shape, jnp.bfloat16),
                pltpu.VMEM(values.shape, jnp.bfloat16),
                pltpu.VMEM((kv_heads, 1, rows), jnp.float32),
                pltpu.SemaphoreType.DMA((2, len(STAGES))),
            ],
            vmem=51,
            name="attend",
        )(scalars, own, other, keys, values)

    with jax.named_scope("merge"):
        packed = kernel_call(
            pair_kernel,
            jax.ShapeDtypeStruct((pieces, PIECE + 8, HEAD_SIZE), jnp.bfloat16),
            [VMEM, VMEM],
            name="pair",
        )(kept, shift(sent, 0, 0, 1))
        chips = [[chip * CORES + core for chip in range(Z * X)] for core in range(CORES)]
        packed = lax.all_to_all(packed, "hst", 0, 0, axis_index_groups=chips)
        attended = kernel_call(
            merge_kernel,
            jax.ShapeDtypeStruct((pieces, PIECE, HEAD_SIZE), jnp.bfloat16),
            [VMEM],
            name="merge",
        )(packed)
        attended = lax.all_to_all(attended, "hst", 0, 0, axis_index_groups=chips)

    with jax.named_scope("project"):
        projected = kernel_call(
            project_kernel,
            jax.ShapeDtypeStruct((tokens // PIECE, PIECE, out_weight.shape[1]), jnp.float32),
            [SMEM] + [VMEM] * 3,
            name="project",
        )(scalars, attended, shift(attended, 0, 0, 1), out_weight)
        shares = lax.axis_size("tensor")
        mine = lax.axis_index("tensor")
        total = lax.dynamic_index_in_dim(projected, mine, 0, keepdims=False)
        for hop in range(1, shares):
            part = lax.dynamic_index_in_dim(projected, (mine + hop) % shares, 0, keepdims=False)
            total += lax.ppermute(part, "tensor", [(i, (i + hop) % shares) for i in range(shares)])
        return total.astype(jnp.bfloat16)


def solution(mesh):
    placed = (
        P("hst", None, "tensor"),
        P("hst", "tensor"),
        P("hst", "tensor"),
        P("hst"),
        P(),
        P("tensor", "hst"),
    )
    return jax.shard_map(
        on_device, mesh=mesh, in_specs=placed, out_specs=P("tensor", "hst"), check_vma=False
    )
```

```python
import functools

import jax
import jax.numpy as jnp
from jax import lax
from jax.experimental import pallas as pl
from jax.experimental.pallas import tpu as pltpu
from jax.sharding import PartitionSpec as P

HEAD_SIZE = 128
PIECE = 16
CHUNK = 1024
STAGES = (0, 1024, 4096)
LOG2E = 1.4426950408889634
SCORE_SCALE = LOG2E * HEAD_SIZE ** (-0.5)
MASKED = -1e30
SAMPLE = 128
SUM_LIMIT = 2.0**64
Z, X, CORES = 8, 4, 2
HBM = pl.BlockSpec(memory_space=pl.ANY)
VMEM = pl.BlockSpec(memory_space=pltpu.VMEM)
SMEM = pl.BlockSpec(memory_space=pltpu.SMEM)


def dot(lhs, rhs, lhs_dim, rhs_dim):
    return lax.dot_general(
        lhs, rhs, (((lhs_dim,), (rhs_dim,)), ((), ())), preferred_element_type=jnp.float32
    )


def attend_kernel(
    scalars_ref, own_ref, other_ref, keys_hbm, values_hbm, kept_ref, sent_ref,
    keys_ref, values_ref, row_max, arrivals,
):
    rows = own_ref.shape[0]
    queries = (own_ref, other_ref)
    results = (kept_ref, sent_ref)
    first_limit = scalars_ref[0]
    last_limit = scalars_ref[1]
    my_core = scalars_ref[2]
    tokens = scalars_ref[3]
    chunks = pl.cdiv(last_limit, CHUNK)

    copies = []
    for stage, (start, stop) in enumerate(zip(STAGES, (*STAGES[1:], keys_hbm.shape[0]))):
        place = pl.ds(start, stop - start)
        copies.append(
            [
                pltpu.make_async_copy(source.at[place], target.at[place], arrivals.at[kind, stage])
                for kind, (source, target) in enumerate(
                    ((keys_hbm, keys_ref), (values_hbm, values_ref))
                )
            ]
        )
        for copy in copies[-1]:
            copy.start()

    def await_stage(stage):
        for copy in copies[stage]:
            copy.wait()

    def column_of(head):
        column = my_core if head == 0 else 1 - my_core
        return pl.ds(pl.multiple_of(column * HEAD_SIZE, HEAD_SIZE), HEAD_SIZE)

    def loop(start, stop, body):
        def one(chunk, carry):
            body(chunk)
            return carry

        lax.fori_loop(start, stop, one, 0)

    def step(chunk, masked, running, first=False):
        base = pl.multiple_of(chunk * CHUNK, CHUNK)
        place = pl.ds(base, CHUNK)
        for head, result in enumerate(results):
            scores = dot(keys_ref[place, column_of(head)], queries[head][...], 1, 1) * SCORE_SCALE
            if masked:
                token = lax.rem(lax.broadcasted_iota(jnp.int32, (1, rows), 1), tokens)
                limit = jnp.minimum(first_limit + token, last_limit)
                slot = lax.broadcasted_iota(jnp.int32, scores.shape, 0) + base
                scores = jnp.where(slot < limit, scores, MASKED)
            if first:
                row_max[head] = jnp.max(scores[:SAMPLE], axis=0, keepdims=True)
            if running:
                before = row_max[head]
                row_max[head] = jnp.maximum(before, jnp.max(scores, axis=0, keepdims=True))
                result[...] *= jnp.exp2(before - row_max[head])
            weights = jnp.exp2(scores - row_max[head]).astype(jnp.bfloat16)
            values = values_ref[place, column_of(head)]
            lhs = jnp.concatenate([values.T, jnp.ones((16, CHUNK), jnp.bfloat16)], axis=0)
            part = dot(lhs, weights, 1, 0)
            result[...] = part if first else result[...] + part

    def arrived_step(chunk, masked):
        for stage, start in enumerate(STAGES[1:], 1):
            pl.when(chunk == start // CHUNK)(functools.partial(await_stage, stage))
        step(chunk, masked, False)

    whole = first_limit // CHUNK
    await_stage(0)
    step(0, False, False, True)
    loop(1, whole, lambda chunk: arrived_step(chunk, False))
    loop(whole, chunks, lambda chunk: arrived_step(chunk, True))
    for stage, start in enumerate(STAGES[1:], 1):
        pl.when(chunks <= start // CHUNK)(functools.partial(await_stage, stage))

    over = jnp.zeros((1, rows), jnp.int32)
    for result in results:
        over += jnp.where(result[HEAD_SIZE : HEAD_SIZE + 1] < SUM_LIMIT, 0, 1)

    @pl.when(jnp.sum(over) > 0)
    def _():
        row_max[...] = jnp.full_like(row_max, MASKED)
        for result in results:
            result[...] = jnp.zeros_like(result)
        loop(0, chunks, lambda chunk: step(chunk, True, True))

    for head, result in enumerate(results):
        result[HEAD_SIZE + 8 :] = jnp.broadcast_to(row_max[head], (8, rows))


def pair_kernel(kept_ref, received_ref, packed_ref):
    rows = kept_ref.shape[1]
    pieces = rows // PIECE
    total_row = slice(HEAD_SIZE, HEAD_SIZE + 1)
    max_row = slice(HEAD_SIZE + 8, HEAD_SIZE + 9)
    peak = jnp.maximum(kept_ref[max_row], received_ref[max_row])
    peak = peak.astype(jnp.bfloat16).astype(jnp.float32)
    kept_factor = jnp.exp2(kept_ref[max_row] - peak)
    received_factor = jnp.exp2(received_ref[max_row] - peak)
    total = kept_ref[total_row] * kept_factor + received_ref[total_row] * received_factor
    out = (
        kept_ref[:HEAD_SIZE] * (kept_factor / total)
        + received_ref[:HEAD_SIZE] * (received_factor / total)
    ).T.astype(jnp.bfloat16)
    high = total.astype(jnp.bfloat16).astype(jnp.float32)
    row = lax.broadcasted_iota(jnp.int32, (pieces, PIECE, HEAD_SIZE), 1)
    lane = lax.broadcasted_iota(jnp.int32, (pieces, PIECE, HEAD_SIZE), 2)

    def spread(value):
        return jnp.broadcast_to(value, (HEAD_SIZE, rows)).T.reshape(pieces, PIECE, HEAD_SIZE)

    stats = jnp.where(lane == row, spread(peak), 0.0)
    stats = jnp.where(lane == row + PIECE, spread(high), stats)
    stats = jnp.where(lane == row + 2 * PIECE, spread(total - high), stats)
    stats = jnp.sum(stats, axis=1, keepdims=True).astype(jnp.bfloat16)
    packed_ref[:, :PIECE] = out.reshape(pieces, PIECE, HEAD_SIZE)
    packed_ref[:, PIECE:] = jnp.broadcast_to(stats, (pieces, 8, HEAD_SIZE))


def take_kernel(scalars_ref, slots_ref, sibling_ref, pieces_ref):
    my_core, root_core = scalars_ref[2], scalars_ref[4]
    tokens, width = slots_ref.shape
    part = width // CORES
    groups = tokens // PIECE
    columns = pl.ds(pl.multiple_of(my_core * part, part), part)

    def cut(source_ref):
        half = source_ref[:, columns]
        for head in range(part // HEAD_SIZE):
            rows = half[:, head * HEAD_SIZE : (head + 1) * HEAD_SIZE]
            pieces_ref[head * groups : (head + 1) * groups] = rows.reshape(groups, PIECE, HEAD_SIZE)

    pl.when(my_core == root_core)(lambda: cut(slots_ref))
    pl.when(my_core != root_core)(lambda: cut(sibling_ref))


def pick_kernel(scalars_ref, received_ref, copies_ref):
    copies_ref[...] = jnp.broadcast_to(received_ref[scalars_ref[5]][None], copies_ref.shape)


def merge_kernel(packed_ref, attended_ref):
    chips = packed_ref.shape[0]
    stats = jnp.max(packed_ref[:, PIECE:].astype(jnp.float32), axis=1).T
    row_max = stats[:PIECE]
    totals = stats[PIECE : 2 * PIECE] + stats[2 * PIECE : 3 * PIECE]
    peak = jnp.max(row_max, axis=1, keepdims=True)
    shares = totals * jnp.exp2(row_max - peak)
    shares = shares / jnp.sum(shares, axis=1, keepdims=True)
    merged = jnp.zeros(attended_ref.shape[1:], jnp.float32)
    for chip in range(chips):
        merged += shares[:, chip : chip + 1] * packed_ref[chip, :PIECE].astype(jnp.float32)
    attended_ref[...] = jnp.broadcast_to(merged.astype(jnp.bfloat16)[None], attended_ref.shape)


def project_kernel(scalars_ref, own_ref, sibling_ref, weight_ref, out_ref):
    my_core = scalars_ref[2]
    groups = out_ref.shape[0]
    heads = own_ref.shape[0] // groups
    depth = heads * HEAD_SIZE
    total = jnp.zeros((groups * PIECE, out_ref.shape[2]), jnp.float32)
    for source, core in ((own_ref, my_core), (sibling_ref, 1 - my_core)):
        lhs = jnp.concatenate(
            [
                source[head * groups : (head + 1) * groups].reshape(-1, HEAD_SIZE)
                for head in range(heads)
            ],
            axis=1,
        )
        total += dot(lhs, weight_ref[pl.ds(pl.multiple_of(core * depth, depth), depth)], 1, 0)
    out_ref[...] = total.reshape(out_ref.shape)


def kernel_call(body, out_shape, in_specs, scratch=(), vmem=40, name=None):
    return pl.pallas_call(
        body,
        out_shape=out_shape,
        in_specs=in_specs,
        out_specs=jax.tree.map(lambda _: VMEM, out_shape),
        scratch_shapes=scratch,
        compiler_params=pltpu.CompilerParams(vmem_limit_bytes=vmem << 20),
        name=name,
    )


def from_sibling(value):
    pairs = [(host, host ^ 1) for host in range(Z * X * CORES)]
    return lax.ppermute(value, "hst", pairs)


def over_chips(value):
    groups = [[chip * CORES + core for chip in range(Z * X)] for core in range(CORES)]
    return lax.all_to_all(value, "hst", 0, 0, axis_index_groups=groups)


def broadcast_queries(slots, scalars):
    tokens, width = slots.shape
    heads = width // HEAD_SIZE // CORES
    shape = jax.ShapeDtypeStruct((heads * tokens // PIECE, PIECE, HEAD_SIZE), slots.dtype)
    pieces = kernel_call(take_kernel, shape, [SMEM, VMEM, VMEM], name="take")(
        scalars, slots, from_sibling(slots)
    )
    copies = kernel_call(pick_kernel, shape, [SMEM, VMEM], name="pick")(
        scalars, over_chips(pieces)
    )
    own = over_chips(copies).reshape(heads * tokens, HEAD_SIZE)
    return own, from_sibling(own)


def on_device(query_slots, keys, values, counts, query_host, out_weight):
    tokens, width = query_slots.shape[1:]
    kv_heads = keys.shape[1] // HEAD_SIZE
    rows = width // keys.shape[1] * tokens
    pieces = rows // PIECE
    root = query_host[0]
    me = lax.axis_index("hst")

    with jax.named_scope("queries"):
        last = counts[0]
        first = jnp.where(me == root, last - tokens + 1, last)
        scalars = jnp.stack(
            [first, last, me % CORES, jnp.int32(tokens), root % CORES, root // CORES]
        )
        own, other = broadcast_queries(query_slots[0], scalars)

    with jax.named_scope("attend"):
        result = jax.ShapeDtypeStruct((HEAD_SIZE + 16, rows), jnp.float32)
        kept, sent = kernel_call(
            attend_kernel,
            (result, result),
            [SMEM, VMEM, VMEM, HBM, HBM],
            [
                pltpu.VMEM(keys.shape, jnp.bfloat16),
                pltpu.VMEM(values.shape, jnp.bfloat16),
                pltpu.VMEM((kv_heads, 1, rows), jnp.float32),
                pltpu.SemaphoreType.DMA((2, len(STAGES))),
            ],
            vmem=51,
            name="attend",
        )(scalars, own, other, keys, values)

    with jax.named_scope("merge"):
        packed = kernel_call(
            pair_kernel,
            jax.ShapeDtypeStruct((pieces, PIECE + 8, HEAD_SIZE), jnp.bfloat16),
            [VMEM, VMEM],
            name="pair",
        )(kept, from_sibling(sent))
        attended = kernel_call(
            merge_kernel,
            jax.ShapeDtypeStruct((pieces, PIECE, HEAD_SIZE), jnp.bfloat16),
            [VMEM],
            name="merge",
        )(over_chips(packed))
        attended = over_chips(attended)

    with jax.named_scope("project"):
        projected = kernel_call(
            project_kernel,
            jax.ShapeDtypeStruct((tokens // PIECE, PIECE, out_weight.shape[1]), jnp.float32),
            [SMEM] + [VMEM] * 3,
            name="project",
        )(scalars, attended, from_sibling(attended), out_weight)
        shares = lax.axis_size("tensor")
        mine = lax.axis_index("tensor")
        total = lax.dynamic_index_in_dim(projected, mine, 0, keepdims=False)
        for hop in range(1, shares):
            part = lax.dynamic_index_in_dim(projected, (mine + hop) % shares, 0, keepdims=False)
            total += lax.ppermute(part, "tensor", [(i, (i + hop) % shares) for i in range(shares)])
        return total.astype(jnp.bfloat16)


def solution(mesh):
    placed = (
        P("hst", None, "tensor"),
        P("hst", "tensor"),
        P("hst", "tensor"),
        P("hst"),
        P(),
        P("tensor", "hst"),
    )
    return jax.shard_map(
        on_device, mesh=mesh, in_specs=placed, out_specs=P("tensor", "hst"), check_vma=False
    )
```

```python
import functools

import jax
import jax.numpy as jnp
from jax import lax
from jax.experimental import pallas as pl
from jax.experimental.pallas import tpu as pltpu
from jax.sharding import PartitionSpec as P

HEAD_SIZE = 128
PIECE = 16
CHUNK = 1024
STAGES = (1024, 2048, 4096)
LOG2E = 1.4426950408889634
SCORE_SCALE = LOG2E * HEAD_SIZE ** (-0.5)
MASKED = -1e30
SAMPLE = 128
SUM_LIMIT = 2.0**64
Z, X, CORES = 8, 4, 2
HBM = pl.BlockSpec(memory_space=pl.ANY)
VMEM = pl.BlockSpec(memory_space=pltpu.VMEM)
SMEM = pl.BlockSpec(memory_space=pltpu.SMEM)


def dot(lhs, rhs, lhs_dim, rhs_dim):
    return lax.dot_general(
        lhs, rhs, (((lhs_dim,), (rhs_dim,)), ((), ())), preferred_element_type=jnp.float32
    )


def attend_kernel(
    scalars_ref, own_ref, other_ref, keys_start_ref, values_start_ref, keys_hbm, values_hbm,
    kept_ref, sent_ref,
    queries, keys_ref, values_ref, row_max, arrivals,
):
    rows = queries.shape[1]
    results = (kept_ref, sent_ref)
    first_limit = scalars_ref[0]
    last_limit = scalars_ref[1]
    my_core = scalars_ref[2]
    my_x = scalars_ref[3]
    chunks = pl.cdiv(last_limit, CHUNK)

    copies = []
    for stage, (start, stop) in enumerate(zip(STAGES, (*STAGES[1:], keys_hbm.shape[0]))):
        place = pl.ds(start, stop - start)
        copies.append(
            [
                pltpu.make_async_copy(source.at[place], target.at[place], arrivals.at[kind, stage])
                for kind, (source, target) in enumerate(
                    ((keys_hbm, keys_ref), (values_hbm, values_ref))
                )
            ]
        )
        for copy in copies[-1]:
            copy.start()

    def await_stage(stage):
        for copy in copies[stage]:
            copy.wait()

    def column_of(head):
        column = my_core if head == 0 else 1 - my_core
        return pl.ds(pl.multiple_of(column * HEAD_SIZE, HEAD_SIZE), HEAD_SIZE)

    def loop(start, stop, body):
        def one(chunk, carry):
            body(chunk)
            return carry

        lax.fori_loop(start, stop, one, 0)

    for head, source in enumerate((own_ref, other_ref)):
        groups, _, columns = source.shape
        tokens = groups * PIECE
        for group in range(groups):
            piece = source[lax.rem(my_x - group + groups, groups)]
            for part in range(columns // HEAD_SIZE):
                queries[head, pl.ds((part * groups + group) * PIECE, PIECE)] = piece[
                    :, part * HEAD_SIZE : (part + 1) * HEAD_SIZE
                ]

    def step(chunk, masked, running, first=False):
        base = pl.multiple_of(chunk * CHUNK, CHUNK)
        place = pl.ds(base, CHUNK)

        def keys_of(column):
            return keys_start_ref[:, column] if first else keys_ref[place, column]

        def values_of(column):
            return values_start_ref[:, column] if first else values_ref[place, column]

        products = [
            dot(keys_of(column_of(head)), queries[head], 1, 1)
            for head in range(len(results))
        ]
        for head, result in enumerate(results):
            scores = products[head] * SCORE_SCALE
            if masked:
                token = lax.rem(lax.broadcasted_iota(jnp.int32, (1, rows), 1), tokens)
                limit = jnp.minimum(first_limit + token, last_limit)
                slot = lax.broadcasted_iota(jnp.int32, scores.shape, 0) + base
                scores = jnp.where(slot < limit, scores, MASKED)
            if first:
                row_max[head] = jnp.max(scores[:SAMPLE], axis=0, keepdims=True)
            if running:
                before = row_max[head]
                row_max[head] = jnp.maximum(before, jnp.max(scores, axis=0, keepdims=True))
                result[...] *= jnp.exp2(before - row_max[head])
            weights = jnp.exp2(scores - row_max[head]).astype(jnp.bfloat16)
            values = values_of(column_of(head))
            lhs = jnp.concatenate([values.T, jnp.ones((16, CHUNK), jnp.bfloat16)], axis=0)
            part = dot(lhs, weights, 1, 0)
            result[...] = part if first else result[...] + part

    def arrived_step(chunk, masked):
        for stage, start in enumerate(STAGES):
            pl.when(chunk == start // CHUNK)(functools.partial(await_stage, stage))
        step(chunk, masked, False)

    whole = first_limit // CHUNK
    step(0, False, False, True)
    loop(1, whole, lambda chunk: arrived_step(chunk, False))
    loop(whole, chunks, lambda chunk: arrived_step(chunk, True))
    for stage, start in enumerate(STAGES):
        pl.when(chunks <= start // CHUNK)(functools.partial(await_stage, stage))

    over = jnp.zeros((1, rows), jnp.int32)
    for result in results:
        over += jnp.where(result[HEAD_SIZE : HEAD_SIZE + 1] < SUM_LIMIT, 0, 1)

    @pl.when(jnp.sum(over) > 0)
    def _():
        for source, target in ((keys_start_ref, keys_ref), (values_start_ref, values_ref)):
            target[:CHUNK] = source[...]
        row_max[...] = jnp.full_like(row_max, MASKED)
        for result in results:
            result[...] = jnp.zeros_like(result)
        loop(0, chunks, lambda chunk: step(chunk, True, True))

    for head, result in enumerate(results):
        result[HEAD_SIZE + 8 :] = jnp.broadcast_to(row_max[head], (8, rows))


def pair_kernel(kept_ref, received_ref, packed_ref):
    rows = kept_ref.shape[1]
    pieces = rows // PIECE
    total_row = slice(HEAD_SIZE, HEAD_SIZE + 1)
    max_row = slice(HEAD_SIZE + 8, HEAD_SIZE + 9)
    peak = jnp.maximum(kept_ref[max_row], received_ref[max_row])
    peak = peak.astype(jnp.bfloat16).astype(jnp.float32)
    kept_factor = jnp.exp2(kept_ref[max_row] - peak)
    received_factor = jnp.exp2(received_ref[max_row] - peak)
    total = kept_ref[total_row] * kept_factor + received_ref[total_row] * received_factor
    out = (
        kept_ref[:HEAD_SIZE] * (kept_factor / total)
        + received_ref[:HEAD_SIZE] * (received_factor / total)
    ).T.astype(jnp.bfloat16)
    high = total.astype(jnp.bfloat16).astype(jnp.float32)
    row = lax.broadcasted_iota(jnp.int32, (pieces, PIECE, HEAD_SIZE), 1)
    lane = lax.broadcasted_iota(jnp.int32, (pieces, PIECE, HEAD_SIZE), 2)

    def spread(value):
        return jnp.broadcast_to(value, (HEAD_SIZE, rows)).T.reshape(pieces, PIECE, HEAD_SIZE)

    stats = jnp.where(lane == row, spread(peak), 0.0)
    stats = jnp.where(lane == row + PIECE, spread(high), stats)
    stats = jnp.where(lane == row + 2 * PIECE, spread(total - high), stats)
    stats = jnp.sum(stats, axis=1, keepdims=True).astype(jnp.bfloat16)
    packed_ref[:, :PIECE] = out.reshape(pieces, PIECE, HEAD_SIZE)
    packed_ref[:, PIECE:] = jnp.broadcast_to(stats, (pieces, 8, HEAD_SIZE))


def repeat_kernel(value_ref, copies_ref):
    copies_ref[...] = jnp.broadcast_to(value_ref[...][None], copies_ref.shape)


def merge_kernel(packed_ref, attended_ref):
    chips = packed_ref.shape[0]
    stats = jnp.max(packed_ref[:, PIECE:].astype(jnp.float32), axis=1).T
    row_max = stats[:PIECE]
    totals = stats[PIECE : 2 * PIECE] + stats[2 * PIECE : 3 * PIECE]
    peak = jnp.max(row_max, axis=1, keepdims=True)
    shares = totals * jnp.exp2(row_max - peak)
    shares = shares / jnp.sum(shares, axis=1, keepdims=True)
    merged = jnp.zeros(attended_ref.shape[1:], jnp.float32)
    for chip in range(chips):
        merged += shares[:, chip : chip + 1] * packed_ref[chip, :PIECE].astype(jnp.float32)
    attended_ref[...] = jnp.broadcast_to(merged.astype(jnp.bfloat16)[None], attended_ref.shape)


def project_kernel(scalars_ref, own_ref, sibling_ref, weight_ref, out_ref):
    my_core = scalars_ref[2]
    groups = out_ref.shape[0]
    heads = own_ref.shape[0] // groups
    depth = heads * HEAD_SIZE
    total = jnp.zeros((groups * PIECE, out_ref.shape[2]), jnp.float32)
    for source, core in ((own_ref, my_core), (sibling_ref, 1 - my_core)):
        lhs = jnp.concatenate(
            [
                source[head * groups : (head + 1) * groups].reshape(-1, HEAD_SIZE)
                for head in range(heads)
            ],
            axis=1,
        )
        total += dot(lhs, weight_ref[pl.ds(pl.multiple_of(core * depth, depth), depth)], 1, 0)
    out_ref[...] = total.reshape(out_ref.shape)


def kernel_call(body, out_shape, in_specs, scratch=(), vmem=40, name=None):
    return pl.pallas_call(
        body,
        out_shape=out_shape,
        in_specs=in_specs,
        out_specs=jax.tree.map(lambda _: VMEM, out_shape),
        scratch_shapes=scratch,
        compiler_params=pltpu.CompilerParams(vmem_limit_bytes=vmem << 20),
        name=name,
    )


def shift(value, dz, dx, dcore):
    def index(z, x, core):
        return ((z % Z) * X + x % X) * CORES + core % CORES

    pairs = [
        (index(z, x, core), index(z + dz, x + dx, core + dcore))
        for z in range(Z)
        for x in range(X)
        for core in range(CORES)
    ]
    return lax.ppermute(value, "hst", pairs)


def gather(value, groups):
    copies = kernel_call(
        repeat_kernel,
        jax.ShapeDtypeStruct((len(groups[0]), *value.shape), value.dtype),
        [VMEM],
        name="repeat",
    )(value)
    return lax.all_to_all(copies, "hst", 0, 0, axis_index_groups=groups)


def broadcast_queries(slots, root, ready):
    me = lax.axis_index("hst")
    core, x = me % CORES, me // CORES % X
    root_core, root_x, root_z = root % CORES, root // CORES % X, root // (CORES * X)
    tokens, width = slots.shape
    part = width // CORES
    own = lax.optimization_barrier(lax.dynamic_slice_in_dim(slots, core * part, part, 1))
    other = lax.dynamic_slice_in_dim(shift(slots, 0, 0, 1), core * part, part, 1)
    half = jnp.where(core == root_core, own, other).reshape(X, tokens // X, part)

    group = lax.dynamic_index_in_dim(half, x, 0, keepdims=False)
    for hop in range(1, X):
        sent = lax.dynamic_index_in_dim(half, (x + hop) % X, 0, keepdims=False)
        group = jnp.where((x - root_x) % X == hop, shift(sent, 0, hop, 0), group)

    columns = [[(z * X + i) * CORES + c for z in range(Z)] for i in range(X) for c in range(CORES)]
    group = lax.dynamic_index_in_dim(gather(group, columns), root_z, 0, keepdims=False)
    group, ready = lax.optimization_barrier((group, ready))

    half = jnp.stack([group] + [shift(group, 0, hop, 0) for hop in range(1, X)])
    return half, shift(half, 0, 0, 1), ready


def on_device(query_slots, keys, values, counts, query_host, out_weight):
    tokens, width = query_slots.shape[1:]
    kv_heads = keys.shape[1] // HEAD_SIZE
    rows = width // keys.shape[1] * tokens
    pieces = rows // PIECE
    root = query_host[0]
    me = lax.axis_index("hst")

    with jax.named_scope("queries"):
        last = counts[0]
        first = jnp.where(me == root, last - tokens + 1, last)
        scalars = jnp.stack([first, last, me % CORES, me // CORES % X])
        own, other, ready = broadcast_queries(
            query_slots[0], root, (scalars, keys[:CHUNK], values[:CHUNK])
        )
        scalars, keys_start, values_start = ready

    with jax.named_scope("attend"):
        result = jax.ShapeDtypeStruct((HEAD_SIZE + 16, rows), jnp.float32)
        kept, sent = kernel_call(
            attend_kernel,
            (result, result),
            [SMEM, VMEM, VMEM, VMEM, VMEM, HBM, HBM],
            [
                pltpu.VMEM((kv_heads, rows, HEAD_SIZE), jnp.bfloat16),
                pltpu.VMEM(keys.shape, jnp.bfloat16),
                pltpu.VMEM(values.shape, jnp.bfloat16),
                pltpu.VMEM((kv_heads, 1, rows), jnp.float32),
                pltpu.SemaphoreType.DMA((2, len(STAGES))),
            ],
            vmem=51,
            name="attend",
        )(scalars, own, other, keys_start, values_start, keys, values)

    with jax.named_scope("merge"):
        packed = kernel_call(
            pair_kernel,
            jax.ShapeDtypeStruct((pieces, PIECE + 8, HEAD_SIZE), jnp.bfloat16),
            [VMEM, VMEM],
            name="pair",
        )(kept, shift(sent, 0, 0, 1))
        chips = [[chip * CORES + core for chip in range(Z * X)] for core in range(CORES)]
        packed = lax.all_to_all(packed, "hst", 0, 0, axis_index_groups=chips)
        attended = kernel_call(
            merge_kernel,
            jax.ShapeDtypeStruct((pieces, PIECE, HEAD_SIZE), jnp.bfloat16),
            [VMEM],
            name="merge",
        )(packed)
        attended = lax.all_to_all(attended, "hst", 0, 0, axis_index_groups=chips)

    with jax.named_scope("project"):
        projected = kernel_call(
            project_kernel,
            jax.ShapeDtypeStruct((tokens // PIECE, PIECE, out_weight.shape[1]), jnp.float32),
            [SMEM] + [VMEM] * 3,
            name="project",
        )(scalars, attended, shift(attended, 0, 0, 1), out_weight)
        shares = lax.axis_size("tensor")
        mine = lax.axis_index("tensor")
        total = lax.dynamic_index_in_dim(projected, mine, 0, keepdims=False)
        for hop in range(1, shares):
            part = lax.dynamic_index_in_dim(projected, (mine + hop) % shares, 0, keepdims=False)
            total += lax.ppermute(part, "tensor", [(i, (i + hop) % shares) for i in range(shares)])
        return total.astype(jnp.bfloat16)


def solution(mesh):
    placed = (
        P("hst", None, "tensor"),
        P("hst", "tensor"),
        P("hst", "tensor"),
        P("hst"),
        P(),
        P("tensor", "hst"),
    )
    return jax.shard_map(
        on_device, mesh=mesh, in_specs=placed, out_specs=P("tensor", "hst"), check_vma=False
    )
```

```python
import functools

import jax
import jax.numpy as jnp
from jax import lax
from jax.experimental import pallas as pl
from jax.experimental.pallas import tpu as pltpu
from jax.sharding import PartitionSpec as P

HEAD_SIZE = 128
PIECE = 16
CHUNK = 1024
STAGES = (1024, 2048, 4096)
LOG2E = 1.4426950408889634
SCORE_SCALE = LOG2E * HEAD_SIZE ** (-0.5)
MASKED = -1e30
SAMPLE = 128
SUM_LIMIT = 2.0**64
Z, X, CORES = 8, 4, 2
HBM = pl.BlockSpec(memory_space=pl.ANY)
VMEM = pl.BlockSpec(memory_space=pltpu.VMEM)
SMEM = pl.BlockSpec(memory_space=pltpu.SMEM)


def dot(lhs, rhs, lhs_dim, rhs_dim):
    return lax.dot_general(
        lhs, rhs, (((lhs_dim,), (rhs_dim,)), ((), ())), preferred_element_type=jnp.float32
    )


def attend_kernel(
    scalars_ref, own_ref, other_ref, keys_start_ref, values_start_ref, keys_hbm, values_hbm,
    kept_ref, sent_ref,
    queries, keys_ref, values_ref, row_max, arrivals,
):
    rows = queries.shape[1]
    results = (kept_ref, sent_ref)
    first_limit = scalars_ref[0]
    last_limit = scalars_ref[1]
    my_core = scalars_ref[2]
    my_x = scalars_ref[3]
    chunks = pl.cdiv(last_limit, CHUNK)

    copies = []
    for stage, (start, stop) in enumerate(zip(STAGES, (*STAGES[1:], keys_hbm.shape[0]))):
        place = pl.ds(start, stop - start)
        copies.append(
            [
                pltpu.make_async_copy(source.at[place], target.at[place], arrivals.at[kind, stage])
                for kind, (source, target) in enumerate(
                    ((keys_hbm, keys_ref), (values_hbm, values_ref))
                )
            ]
        )
        for copy in copies[-1]:
            copy.start()

    def await_stage(stage):
        for copy in copies[stage]:
            copy.wait()

    def column_of(head):
        column = my_core if head == 0 else 1 - my_core
        return pl.ds(pl.multiple_of(column * HEAD_SIZE, HEAD_SIZE), HEAD_SIZE)

    def loop(start, stop, body):
        def one(chunk, carry):
            body(chunk)
            return carry

        lax.fori_loop(start, stop, one, 0)

    for head, source in enumerate((own_ref, other_ref)):
        groups, _, columns = source.shape
        tokens = groups * PIECE
        for group in range(groups):
            piece = source[lax.rem(my_x - group + groups, groups)]
            for part in range(columns // HEAD_SIZE):
                queries[head, pl.ds((part * groups + group) * PIECE, PIECE)] = piece[
                    :, part * HEAD_SIZE : (part + 1) * HEAD_SIZE
                ]

    def step(chunk, masked, running, first=False):
        base = pl.multiple_of(chunk * CHUNK, CHUNK)
        place = pl.ds(base, CHUNK)

        def keys_of(column):
            return keys_start_ref[:, column] if first else keys_ref[place, column]

        def values_of(column):
            return values_start_ref[:, column] if first else values_ref[place, column]

        products = [
            dot(keys_of(column_of(head)), queries[head], 1, 1)
            for head in range(len(results))
        ]
        for head, result in enumerate(results):
            scores = products[head] * SCORE_SCALE
            if masked:
                token = lax.rem(lax.broadcasted_iota(jnp.int32, (1, rows), 1), tokens)
                limit = jnp.minimum(first_limit + token, last_limit)
                slot = lax.broadcasted_iota(jnp.int32, scores.shape, 0) + base
                scores = jnp.where(slot < limit, scores, MASKED)
            if first:
                row_max[head] = jnp.max(scores[:SAMPLE], axis=0, keepdims=True)
            if running:
                before = row_max[head]
                row_max[head] = jnp.maximum(before, jnp.max(scores, axis=0, keepdims=True))
                result[...] *= jnp.exp2(before - row_max[head])
            weights = jnp.exp2(scores - row_max[head]).astype(jnp.bfloat16)
            values = values_of(column_of(head))
            lhs = jnp.concatenate([values.T, jnp.ones((16, CHUNK), jnp.bfloat16)], axis=0)
            part = dot(lhs, weights, 1, 0)
            result[...] = part if first else result[...] + part

    def arrived_step(chunk, masked):
        for stage, start in enumerate(STAGES):
            pl.when(chunk == start // CHUNK)(functools.partial(await_stage, stage))
        step(chunk, masked, False)

    whole = first_limit // CHUNK
    step(0, False, False, True)
    loop(1, whole, lambda chunk: arrived_step(chunk, False))
    loop(whole, chunks, lambda chunk: arrived_step(chunk, True))
    for stage, start in enumerate(STAGES):
        pl.when(chunks <= start // CHUNK)(functools.partial(await_stage, stage))

    over = jnp.zeros((1, rows), jnp.int32)
    for result in results:
        over += jnp.where(result[HEAD_SIZE : HEAD_SIZE + 1] < SUM_LIMIT, 0, 1)

    @pl.when(jnp.sum(over) > 0)
    def _():
        for source, target in ((keys_start_ref, keys_ref), (values_start_ref, values_ref)):
            target[:CHUNK] = source[...]
        row_max[...] = jnp.full_like(row_max, MASKED)
        for result in results:
            result[...] = jnp.zeros_like(result)
        loop(0, chunks, lambda chunk: step(chunk, True, True))

    for head, result in enumerate(results):
        result[HEAD_SIZE + 8 :] = jnp.broadcast_to(row_max[head], (8, rows))


def pair_kernel(kept_ref, received_ref, packed_ref):
    rows = kept_ref.shape[1]
    pieces = rows // PIECE
    total_row = slice(HEAD_SIZE, HEAD_SIZE + 1)
    max_row = slice(HEAD_SIZE + 8, HEAD_SIZE + 9)
    peak = jnp.maximum(kept_ref[max_row], received_ref[max_row])
    peak = peak.astype(jnp.bfloat16).astype(jnp.float32)
    kept_factor = jnp.exp2(kept_ref[max_row] - peak)
    received_factor = jnp.exp2(received_ref[max_row] - peak)
    total = kept_ref[total_row] * kept_factor + received_ref[total_row] * received_factor
    out = (
        kept_ref[:HEAD_SIZE] * (kept_factor / total)
        + received_ref[:HEAD_SIZE] * (received_factor / total)
    ).T.astype(jnp.bfloat16)
    high = total.astype(jnp.bfloat16).astype(jnp.float32)
    row = lax.broadcasted_iota(jnp.int32, (pieces, PIECE, HEAD_SIZE), 1)
    lane = lax.broadcasted_iota(jnp.int32, (pieces, PIECE, HEAD_SIZE), 2)

    def spread(value):
        return jnp.broadcast_to(value, (HEAD_SIZE, rows)).T.reshape(pieces, PIECE, HEAD_SIZE)

    stats = jnp.where(lane == row, spread(peak), 0.0)
    stats = jnp.where(lane == row + PIECE, spread(high), stats)
    stats = jnp.where(lane == row + 2 * PIECE, spread(total - high), stats)
    stats = jnp.sum(stats, axis=1, keepdims=True).astype(jnp.bfloat16)
    packed_ref[:, :PIECE] = out.reshape(pieces, PIECE, HEAD_SIZE)
    packed_ref[:, PIECE:] = jnp.broadcast_to(stats, (pieces, 8, HEAD_SIZE))


def repeat_kernel(value_ref, copies_ref):
    copies_ref[...] = jnp.broadcast_to(value_ref[...][None], copies_ref.shape)


def merge_kernel(packed_ref, attended_ref):
    chips = packed_ref.shape[0]
    stats = jnp.max(packed_ref[:, PIECE:].astype(jnp.float32), axis=1).T
    row_max = stats[:PIECE]
    totals = stats[PIECE : 2 * PIECE] + stats[2 * PIECE : 3 * PIECE]
    peak = jnp.max(row_max, axis=1, keepdims=True)
    shares = totals * jnp.exp2(row_max - peak)
    shares = shares / jnp.sum(shares, axis=1, keepdims=True)
    merged = jnp.zeros(attended_ref.shape[1:], jnp.float32)
    for chip in range(chips):
        merged += shares[:, chip : chip + 1] * packed_ref[chip, :PIECE].astype(jnp.float32)
    attended_ref[...] = jnp.broadcast_to(merged.astype(jnp.bfloat16)[None], attended_ref.shape)


def project_kernel(own_ref, sibling_ref, weight_ref, out_ref):
    my_core = lax.axis_index("hst") % CORES
    groups = out_ref.shape[0]
    heads = own_ref.shape[0] // groups
    depth = heads * HEAD_SIZE
    total = jnp.zeros((groups * PIECE, out_ref.shape[2]), jnp.float32)
    for source, core in ((own_ref, my_core), (sibling_ref, 1 - my_core)):
        lhs = jnp.concatenate(
            [
                source[head * groups : (head + 1) * groups].reshape(-1, HEAD_SIZE)
                for head in range(heads)
            ],
            axis=1,
        )
        total += dot(lhs, weight_ref[pl.ds(pl.multiple_of(core * depth, depth), depth)], 1, 0)
    out_ref[...] = total.reshape(out_ref.shape)


def sum_kernel(*refs):
    *part_refs, out_ref = refs
    out_ref[...] = sum(part_ref[...] for part_ref in part_refs).astype(out_ref.dtype)


def kernel_call(body, out_shape, in_specs, scratch=(), vmem=40, name=None):
    return pl.pallas_call(
        body,
        out_shape=out_shape,
        in_specs=in_specs,
        out_specs=jax.tree.map(lambda _: VMEM, out_shape),
        scratch_shapes=scratch,
        compiler_params=pltpu.CompilerParams(vmem_limit_bytes=vmem << 20),
        name=name,
    )


def shift(value, dz, dx, dcore):
    def index(z, x, core):
        return ((z % Z) * X + x % X) * CORES + core % CORES

    pairs = [
        (index(z, x, core), index(z + dz, x + dx, core + dcore))
        for z in range(Z)
        for x in range(X)
        for core in range(CORES)
    ]
    return lax.ppermute(value, "hst", pairs)


def gather(value, groups):
    copies = jnp.broadcast_to(value[None], (len(groups[0]), *value.shape))
    return lax.all_to_all(copies, "hst", 0, 0, axis_index_groups=groups)


def broadcast_queries(slots, root, ready):
    me = lax.axis_index("hst")
    core, x = me % CORES, me // CORES % X
    root_core, root_x, root_z = root % CORES, root // CORES % X, root // (CORES * X)
    tokens, width = slots.shape
    part = width // CORES
    own = lax.optimization_barrier(lax.dynamic_slice_in_dim(slots, core * part, part, 1))
    other = lax.dynamic_slice_in_dim(shift(slots, 0, 0, 1), core * part, part, 1)
    half = jnp.where(core == root_core, own, other).reshape(X, tokens // X, part)

    group = lax.dynamic_index_in_dim(half, x, 0, keepdims=False)
    for hop in range(1, X):
        sent = lax.dynamic_index_in_dim(half, (x + hop) % X, 0, keepdims=False)
        group = jnp.where((x - root_x) % X == hop, shift(sent, 0, hop, 0), group)

    columns = [[(z * X + i) * CORES + c for z in range(Z)] for i in range(X) for c in range(CORES)]
    group = lax.dynamic_index_in_dim(gather(group, columns), root_z, 0, keepdims=False)
    group, ready = lax.optimization_barrier((group, ready))

    half = jnp.stack([group] + [shift(group, 0, hop, 0) for hop in range(1, X)])
    return half, shift(half, 0, 0, 1), ready


def on_device(query_slots, keys, values, counts, query_host, out_weight):
    tokens, width = query_slots.shape[1:]
    kv_heads = keys.shape[1] // HEAD_SIZE
    rows = width // keys.shape[1] * tokens
    pieces = rows // PIECE
    root = query_host[0]
    me = lax.axis_index("hst")

    with jax.named_scope("queries"):
        last = counts[0]
        first = jnp.where(me == root, last - tokens + 1, last)
        scalars = jnp.stack([first, last, me % CORES, me // CORES % X])
        own, other, ready = broadcast_queries(
            query_slots[0], root, (scalars, keys[:CHUNK], values[:CHUNK])
        )
        scalars, keys_start, values_start = ready

    with jax.named_scope("attend"):
        result = jax.ShapeDtypeStruct((HEAD_SIZE + 16, rows), jnp.float32)
        kept, sent = kernel_call(
            attend_kernel,
            (result, result),
            [SMEM, VMEM, VMEM, VMEM, VMEM, HBM, HBM],
            [
                pltpu.VMEM((kv_heads, rows, HEAD_SIZE), jnp.bfloat16),
                pltpu.VMEM(keys.shape, jnp.bfloat16),
                pltpu.VMEM(values.shape, jnp.bfloat16),
                pltpu.VMEM((kv_heads, 1, rows), jnp.float32),
                pltpu.SemaphoreType.DMA((2, len(STAGES))),
            ],
            vmem=51,
            name="attend",
        )(scalars, own, other, keys_start, values_start, keys, values)

    with jax.named_scope("merge"):
        packed = kernel_call(
            pair_kernel,
            jax.ShapeDtypeStruct((pieces, PIECE + 8, HEAD_SIZE), jnp.bfloat16),
            [VMEM, VMEM],
            name="pair",
        )(kept, shift(sent, 0, 0, 1))
        chips = [[chip * CORES + core for chip in range(Z * X)] for core in range(CORES)]
        packed = lax.all_to_all(packed, "hst", 0, 0, axis_index_groups=chips)
        attended = kernel_call(
            merge_kernel,
            jax.ShapeDtypeStruct((pieces, PIECE, HEAD_SIZE), jnp.bfloat16),
            [VMEM],
            name="merge",
        )(packed)
        attended = lax.all_to_all(attended, "hst", 0, 0, axis_index_groups=chips)

    with jax.named_scope("project"):
        projected = kernel_call(
            project_kernel,
            jax.ShapeDtypeStruct((tokens // PIECE, PIECE, out_weight.shape[1]), jnp.float32),
            [VMEM] * 3,
            name="project",
        )(attended, shift(attended, 0, 0, 1), out_weight)
        shares = lax.axis_size("tensor")
        mine = lax.axis_index("tensor")
        parts = [lax.dynamic_index_in_dim(projected, mine, 0, keepdims=False)]
        for hop in range(1, shares):
            part = lax.dynamic_index_in_dim(projected, (mine + hop) % shares, 0, keepdims=False)
            parts.append(
                lax.ppermute(part, "tensor", [(k, (k + hop) % shares) for k in range(shares)])
            )
        return kernel_call(
            sum_kernel,
            jax.ShapeDtypeStruct(parts[0].shape, jnp.bfloat16),
            [VMEM] * shares,
            name="sum",
        )(*parts)


def solution(mesh):
    placed = (
        P("hst", None, "tensor"),
        P("hst", "tensor"),
        P("hst", "tensor"),
        P("hst"),
        P(),
        P("tensor", "hst"),
    )
    return jax.shard_map(
        on_device, mesh=mesh, in_specs=placed, out_specs=P("tensor", "hst"), check_vma=False
    )
```

```python
import functools

import jax
import jax.numpy as jnp
from jax import lax
from jax.experimental import pallas as pl
from jax.experimental.pallas import tpu as pltpu
from jax.sharding import PartitionSpec as P

HEAD_SIZE = 128
PIECE = 16
CHUNK = 1024
STAGES = (1024, 2048, 4096)
LOG2E = 1.4426950408889634
SCORE_SCALE = LOG2E * HEAD_SIZE ** (-0.5)
MASKED = -1e30
SAMPLE = 128
SUM_LIMIT = 2.0**64
Z, X, CORES = 8, 4, 2
HBM = pl.BlockSpec(memory_space=pl.ANY)
VMEM = pl.BlockSpec(memory_space=pltpu.VMEM)
SMEM = pl.BlockSpec(memory_space=pltpu.SMEM)


def dot(lhs, rhs, lhs_dim, rhs_dim):
    return lax.dot_general(
        lhs, rhs, (((lhs_dim,), (rhs_dim,)), ((), ())), preferred_element_type=jnp.float32
    )


def attend_kernel(
    scalars_ref, own_ref, other_ref, keys_start_ref, values_start_ref, keys_hbm, values_hbm,
    kept_ref, sent_ref,
    queries, keys_ref, values_ref, row_max, arrivals,
):
    rows = queries.shape[1]
    results = (kept_ref, sent_ref)
    first_limit = scalars_ref[0]
    last_limit = scalars_ref[1]
    my_core = scalars_ref[2]
    my_x = scalars_ref[3]
    chunks = pl.cdiv(last_limit, CHUNK)

    copies = []
    for stage, (start, stop) in enumerate(zip(STAGES, (*STAGES[1:], keys_hbm.shape[0]))):
        place = pl.ds(start, stop - start)
        copies.append(
            [
                pltpu.make_async_copy(source.at[place], target.at[place], arrivals.at[kind, stage])
                for kind, (source, target) in enumerate(
                    ((keys_hbm, keys_ref), (values_hbm, values_ref))
                )
            ]
        )
        for copy in copies[-1]:
            copy.start()

    def await_stage(stage):
        for copy in copies[stage]:
            copy.wait()

    def column_of(head):
        column = my_core if head == 0 else 1 - my_core
        return pl.ds(pl.multiple_of(column * HEAD_SIZE, HEAD_SIZE), HEAD_SIZE)

    def loop(start, stop, body):
        def one(chunk, carry):
            body(chunk)
            return carry

        lax.fori_loop(start, stop, one, 0)

    for head, source in enumerate((own_ref, other_ref)):
        groups, _, columns = source.shape
        tokens = groups * PIECE
        for group in range(groups):
            piece = source[lax.rem(my_x - group + groups, groups)]
            for part in range(columns // HEAD_SIZE):
                queries[head, pl.ds((part * groups + group) * PIECE, PIECE)] = piece[
                    :, part * HEAD_SIZE : (part + 1) * HEAD_SIZE
                ]

    def step(chunk, masked, running, first=False):
        base = pl.multiple_of(chunk * CHUNK, CHUNK)
        place = pl.ds(base, CHUNK)

        def keys_of(column):
            return keys_start_ref[:, column] if first else keys_ref[place, column]

        def values_of(column):
            return values_start_ref[:, column] if first else values_ref[place, column]

        products = [
            dot(keys_of(column_of(head)), queries[head], 1, 1)
            for head in range(len(results))
        ]
        for head, result in enumerate(results):
            scores = products[head] * SCORE_SCALE
            if masked:
                token = lax.rem(lax.broadcasted_iota(jnp.int32, (1, rows), 1), tokens)
                limit = jnp.minimum(first_limit + token, last_limit)
                slot = lax.broadcasted_iota(jnp.int32, scores.shape, 0) + base
                scores = jnp.where(slot < limit, scores, MASKED)
            if first:
                row_max[head] = jnp.max(scores[:SAMPLE], axis=0, keepdims=True)
            if running:
                before = row_max[head]
                row_max[head] = jnp.maximum(before, jnp.max(scores, axis=0, keepdims=True))
                result[...] *= jnp.exp2(before - row_max[head])
            weights = jnp.exp2(scores - row_max[head]).astype(jnp.bfloat16)
            values = values_of(column_of(head))
            lhs = jnp.concatenate([values.T, jnp.ones((16, CHUNK), jnp.bfloat16)], axis=0)
            part = dot(lhs, weights, 1, 0)
            result[...] = part if first else result[...] + part

    def arrived_step(chunk, masked):
        for stage, start in enumerate(STAGES):
            pl.when(chunk == start // CHUNK)(functools.partial(await_stage, stage))
        step(chunk, masked, False)

    whole = first_limit // CHUNK
    step(0, False, False, True)
    loop(1, whole, lambda chunk: arrived_step(chunk, False))
    loop(whole, chunks, lambda chunk: arrived_step(chunk, True))
    for stage, start in enumerate(STAGES):
        pl.when(chunks <= start // CHUNK)(functools.partial(await_stage, stage))

    over = jnp.zeros((1, rows), jnp.int32)
    for result in results:
        over += jnp.where(result[HEAD_SIZE : HEAD_SIZE + 1] < SUM_LIMIT, 0, 1)

    @pl.when(jnp.sum(over) > 0)
    def _():
        for source, target in ((keys_start_ref, keys_ref), (values_start_ref, values_ref)):
            target[:CHUNK] = source[...]
        row_max[...] = jnp.full_like(row_max, MASKED)
        for result in results:
            result[...] = jnp.zeros_like(result)
        loop(0, chunks, lambda chunk: step(chunk, True, True))

    for head, result in enumerate(results):
        result[HEAD_SIZE + 8 :] = jnp.broadcast_to(row_max[head], (8, rows))


def pair_kernel(kept_ref, received_ref, packed_ref):
    rows = kept_ref.shape[1]
    pieces = rows // PIECE
    total_row = slice(HEAD_SIZE, HEAD_SIZE + 1)
    max_row = slice(HEAD_SIZE + 8, HEAD_SIZE + 9)
    peak = jnp.maximum(kept_ref[max_row], received_ref[max_row])
    peak = peak.astype(jnp.bfloat16).astype(jnp.float32)
    kept_factor = jnp.exp2(kept_ref[max_row] - peak)
    received_factor = jnp.exp2(received_ref[max_row] - peak)
    total = kept_ref[total_row] * kept_factor + received_ref[total_row] * received_factor
    out = (
        kept_ref[:HEAD_SIZE] * (kept_factor / total)
        + received_ref[:HEAD_SIZE] * (received_factor / total)
    ).T.astype(jnp.bfloat16)
    high = total.astype(jnp.bfloat16).astype(jnp.float32)
    row = lax.broadcasted_iota(jnp.int32, (pieces, PIECE, HEAD_SIZE), 1)
    lane = lax.broadcasted_iota(jnp.int32, (pieces, PIECE, HEAD_SIZE), 2)

    def spread(value):
        return jnp.broadcast_to(value, (HEAD_SIZE, rows)).T.reshape(pieces, PIECE, HEAD_SIZE)

    stats = jnp.where(lane == row, spread(peak), 0.0)
    stats = jnp.where(lane == row + PIECE, spread(high), stats)
    stats = jnp.where(lane == row + 2 * PIECE, spread(total - high), stats)
    stats = jnp.sum(stats, axis=1, keepdims=True).astype(jnp.bfloat16)
    packed_ref[:, :PIECE] = out.reshape(pieces, PIECE, HEAD_SIZE)
    packed_ref[:, PIECE:] = jnp.broadcast_to(stats, (pieces, 8, HEAD_SIZE))


def repeat_kernel(value_ref, copies_ref):
    copies_ref[...] = jnp.broadcast_to(value_ref[...][None], copies_ref.shape)


def merge_kernel(packed_ref, attended_ref):
    chips = packed_ref.shape[0]
    stats = jnp.max(packed_ref[:, PIECE:].astype(jnp.float32), axis=1).T
    row_max = stats[:PIECE]
    totals = stats[PIECE : 2 * PIECE] + stats[2 * PIECE : 3 * PIECE]
    peak = jnp.max(row_max, axis=1, keepdims=True)
    shares = totals * jnp.exp2(row_max - peak)
    shares = shares / jnp.sum(shares, axis=1, keepdims=True)
    merged = jnp.zeros(attended_ref.shape[1:], jnp.float32)
    for chip in range(chips):
        merged += shares[:, chip : chip + 1] * packed_ref[chip, :PIECE].astype(jnp.float32)
    attended_ref[...] = jnp.broadcast_to(merged.astype(jnp.bfloat16)[None], attended_ref.shape)


def project_kernel(core, pieces_ref, weight_ref, *refs):
    *before, out_ref = refs
    half = core(lax.axis_index("hst") % CORES)
    groups = out_ref.shape[0]
    heads = pieces_ref.shape[0] // groups
    depth = heads * HEAD_SIZE
    lhs = jnp.concatenate(
        [
            pieces_ref[head * groups : (head + 1) * groups].reshape(-1, HEAD_SIZE)
            for head in range(heads)
        ],
        axis=1,
    )
    product = dot(lhs, weight_ref[pl.ds(pl.multiple_of(half * depth, depth), depth)], 1, 0)
    product = product.reshape(out_ref.shape)
    out_ref[...] = product + before[0][...] if before else product


def sum_kernel(*refs):
    *part_refs, out_ref = refs
    out_ref[...] = sum(part_ref[...] for part_ref in part_refs).astype(out_ref.dtype)


def kernel_call(body, out_shape, in_specs, scratch=(), vmem=40, name=None):
    return pl.pallas_call(
        body,
        out_shape=out_shape,
        in_specs=in_specs,
        out_specs=jax.tree.map(lambda _: VMEM, out_shape),
        scratch_shapes=scratch,
        compiler_params=pltpu.CompilerParams(vmem_limit_bytes=vmem << 20),
        name=name,
    )


def shift(value, dz, dx, dcore):
    def index(z, x, core):
        return ((z % Z) * X + x % X) * CORES + core % CORES

    pairs = [
        (index(z, x, core), index(z + dz, x + dx, core + dcore))
        for z in range(Z)
        for x in range(X)
        for core in range(CORES)
    ]
    return lax.ppermute(value, "hst", pairs)


def gather(value, groups):
    copies = jnp.broadcast_to(value[None], (len(groups[0]), *value.shape))
    return lax.all_to_all(copies, "hst", 0, 0, axis_index_groups=groups)


def broadcast_queries(slots, root, ready):
    me = lax.axis_index("hst")
    core, x = me % CORES, me // CORES % X
    root_core, root_x, root_z = root % CORES, root // CORES % X, root // (CORES * X)
    tokens, width = slots.shape
    part = width // CORES
    own = lax.optimization_barrier(lax.dynamic_slice_in_dim(slots, core * part, part, 1))
    other = lax.dynamic_slice_in_dim(shift(slots, 0, 0, 1), core * part, part, 1)
    half = jnp.where(core == root_core, own, other).reshape(X, tokens // X, part)

    group = lax.dynamic_index_in_dim(half, x, 0, keepdims=False)
    for hop in range(1, X):
        sent = lax.dynamic_index_in_dim(half, (x + hop) % X, 0, keepdims=False)
        group = jnp.where((x - root_x) % X == hop, shift(sent, 0, hop, 0), group)

    columns = [[(z * X + i) * CORES + c for z in range(Z)] for i in range(X) for c in range(CORES)]
    group = lax.dynamic_index_in_dim(gather(group, columns), root_z, 0, keepdims=False)
    group, ready = lax.optimization_barrier((group, ready))

    half = jnp.stack([group] + [shift(group, 0, hop, 0) for hop in range(1, X)])
    return half, shift(half, 0, 0, 1), ready


def on_device(query_slots, keys, values, counts, query_host, out_weight):
    tokens, width = query_slots.shape[1:]
    kv_heads = keys.shape[1] // HEAD_SIZE
    rows = width // keys.shape[1] * tokens
    pieces = rows // PIECE
    root = query_host[0]
    me = lax.axis_index("hst")

    with jax.named_scope("queries"):
        last = counts[0]
        first = jnp.where(me == root, last - tokens + 1, last)
        scalars = jnp.stack([first, last, me % CORES, me // CORES % X])
        own, other, ready = broadcast_queries(
            query_slots[0], root, (scalars, keys[:CHUNK], values[:CHUNK])
        )
        scalars, keys_start, values_start = ready

    with jax.named_scope("attend"):
        result = jax.ShapeDtypeStruct((HEAD_SIZE + 16, rows), jnp.float32)
        kept, sent = kernel_call(
            attend_kernel,
            (result, result),
            [SMEM, VMEM, VMEM, VMEM, VMEM, HBM, HBM],
            [
                pltpu.VMEM((kv_heads, rows, HEAD_SIZE), jnp.bfloat16),
                pltpu.VMEM(keys.shape, jnp.bfloat16),
                pltpu.VMEM(values.shape, jnp.bfloat16),
                pltpu.VMEM((kv_heads, 1, rows), jnp.float32),
                pltpu.SemaphoreType.DMA((2, len(STAGES))),
            ],
            vmem=51,
            name="attend",
        )(scalars, own, other, keys_start, values_start, keys, values)

    with jax.named_scope("merge"):
        packed = kernel_call(
            pair_kernel,
            jax.ShapeDtypeStruct((pieces, PIECE + 8, HEAD_SIZE), jnp.bfloat16),
            [VMEM, VMEM],
            name="pair",
        )(kept, shift(sent, 0, 0, 1))
        chips = [[chip * CORES + core for chip in range(Z * X)] for core in range(CORES)]
        packed = lax.all_to_all(packed, "hst", 0, 0, axis_index_groups=chips)
        attended = kernel_call(
            merge_kernel,
            jax.ShapeDtypeStruct((pieces, PIECE, HEAD_SIZE), jnp.bfloat16),
            [VMEM],
            name="merge",
        )(packed)
        attended = lax.all_to_all(attended, "hst", 0, 0, axis_index_groups=chips)

    with jax.named_scope("project"):
        shape = jax.ShapeDtypeStruct((tokens // PIECE, PIECE, out_weight.shape[1]), jnp.float32)
        sibling = shift(attended, 0, 0, 1)
        projected = kernel_call(
            functools.partial(project_kernel, lambda core: core),
            shape,
            [VMEM] * 2,
            name="project_own",
        )(attended, out_weight)
        projected = kernel_call(
            functools.partial(project_kernel, lambda core: 1 - core),
            shape,
            [VMEM] * 3,
            name="project_sibling",
        )(sibling, out_weight, projected)
        shares = lax.axis_size("tensor")
        mine = lax.axis_index("tensor")
        parts = [lax.dynamic_index_in_dim(projected, mine, 0, keepdims=False)]
        for hop in range(1, shares):
            part = lax.dynamic_index_in_dim(projected, (mine + hop) % shares, 0, keepdims=False)
            parts.append(
                lax.ppermute(part, "tensor", [(k, (k + hop) % shares) for k in range(shares)])
            )
        return kernel_call(
            sum_kernel,
            jax.ShapeDtypeStruct(parts[0].shape, jnp.bfloat16),
            [VMEM] * shares,
            name="sum",
        )(*parts)


def solution(mesh):
    placed = (
        P("hst", None, "tensor"),
        P("hst", "tensor"),
        P("hst", "tensor"),
        P("hst"),
        P(),
        P("tensor", "hst"),
    )
    return jax.shard_map(
        on_device, mesh=mesh, in_specs=placed, out_specs=P("tensor", "hst"), check_vma=False
    )
```

```python
import functools

import jax
import jax.numpy as jnp
from jax import lax
from jax.experimental import pallas as pl
from jax.experimental.pallas import tpu as pltpu
from jax.sharding import PartitionSpec as P

HEAD_SIZE = 128
PIECE = 16
CHUNK = 1024
STAGES = (1024, 2048, 4096)
LOG2E = 1.4426950408889634
SCORE_SCALE = LOG2E * HEAD_SIZE ** (-0.5)
MASKED = -1e30
SAMPLE = 16
SUM_LIMIT = 2.0**64
Z, X, CORES = 8, 4, 2
HBM = pl.BlockSpec(memory_space=pl.ANY)
VMEM = pl.BlockSpec(memory_space=pltpu.VMEM)
SMEM = pl.BlockSpec(memory_space=pltpu.SMEM)


def dot(lhs, rhs, lhs_dim, rhs_dim):
    return lax.dot_general(
        lhs, rhs, (((lhs_dim,), (rhs_dim,)), ((), ())), preferred_element_type=jnp.float32
    )


def attend_kernel(
    scalars_ref, own_ref, other_ref, keys_start_ref, values_start_ref, keys_hbm, values_hbm,
    kept_ref, sent_ref,
    queries, keys_ref, values_ref, row_max, arrivals,
):
    rows = queries.shape[1]
    results = (kept_ref, sent_ref)
    first_limit = scalars_ref[0]
    last_limit = scalars_ref[1]
    my_core = scalars_ref[2]
    my_x = scalars_ref[3]
    chunks = pl.cdiv(last_limit, CHUNK)

    copies = []
    for stage, (start, stop) in enumerate(zip(STAGES, (*STAGES[1:], keys_hbm.shape[0]))):
        place = pl.ds(start, stop - start)
        copies.append(
            [
                pltpu.make_async_copy(source.at[place], target.at[place], arrivals.at[kind, stage])
                for kind, (source, target) in enumerate(
                    ((keys_hbm, keys_ref), (values_hbm, values_ref))
                )
            ]
        )
        for copy in copies[-1]:
            copy.start()

    def await_stage(stage):
        for copy in copies[stage]:
            copy.wait()

    def column_of(head):
        column = my_core if head == 0 else 1 - my_core
        return pl.ds(pl.multiple_of(column * HEAD_SIZE, HEAD_SIZE), HEAD_SIZE)

    def loop(start, stop, body):
        def one(chunk, carry):
            body(chunk)
            return carry

        lax.fori_loop(start, stop, one, 0)

    for head, source in enumerate((own_ref, other_ref)):
        groups, _, columns = source.shape
        tokens = groups * PIECE
        for group in range(groups):
            piece = source[lax.rem(my_x - group + groups, groups)]
            for part in range(columns // HEAD_SIZE):
                queries[head, pl.ds((part * groups + group) * PIECE, PIECE)] = piece[
                    :, part * HEAD_SIZE : (part + 1) * HEAD_SIZE
                ]

    def step(chunk, masked, running, first=False):
        base = pl.multiple_of(chunk * CHUNK, CHUNK)
        place = pl.ds(base, CHUNK)

        def keys_of(column):
            return keys_start_ref[:, column] if first else keys_ref[place, column]

        def values_of(column):
            return values_start_ref[:, column] if first else values_ref[place, column]

        products = [
            dot(keys_of(column_of(head)), queries[head], 1, 1)
            for head in range(len(results))
        ]
        for head, result in enumerate(results):
            scores = products[head] * SCORE_SCALE
            if masked:
                token = lax.rem(lax.broadcasted_iota(jnp.int32, (1, rows), 1), tokens)
                limit = jnp.minimum(first_limit + token, last_limit)
                slot = lax.broadcasted_iota(jnp.int32, scores.shape, 0) + base
                scores = jnp.where(slot < limit, scores, MASKED)
            if first:
                row_max[head] = jnp.max(scores[:SAMPLE], axis=0, keepdims=True)
            if running:
                before = row_max[head]
                row_max[head] = jnp.maximum(before, jnp.max(scores, axis=0, keepdims=True))
                result[...] *= jnp.exp2(before - row_max[head])
            weights = jnp.exp2(scores - row_max[head]).astype(jnp.bfloat16)
            values = values_of(column_of(head))
            lhs = jnp.concatenate([values.T, jnp.ones((16, CHUNK), jnp.bfloat16)], axis=0)
            part = dot(lhs, weights, 1, 0)
            result[...] = part if first else result[...] + part

    def arrived_step(chunk, masked):
        for stage, start in enumerate(STAGES):
            pl.when(chunk == start // CHUNK)(functools.partial(await_stage, stage))
        step(chunk, masked, False)

    whole = first_limit // CHUNK
    step(0, False, False, True)
    loop(1, whole, lambda chunk: arrived_step(chunk, False))
    loop(whole, chunks, lambda chunk: arrived_step(chunk, True))
    for stage, start in enumerate(STAGES):
        pl.when(chunks <= start // CHUNK)(functools.partial(await_stage, stage))

    over = jnp.zeros((1, rows), jnp.int32)
    for result in results:
        over += jnp.where(result[HEAD_SIZE : HEAD_SIZE + 1] < SUM_LIMIT, 0, 1)

    @pl.when(jnp.sum(over) > 0)
    def _():
        for source, target in ((keys_start_ref, keys_ref), (values_start_ref, values_ref)):
            target[:CHUNK] = source[...]
        row_max[...] = jnp.full_like(row_max, MASKED)
        for result in results:
            result[...] = jnp.zeros_like(result)
        loop(0, chunks, lambda chunk: step(chunk, True, True))

    for head, result in enumerate(results):
        result[HEAD_SIZE + 8 :] = jnp.broadcast_to(row_max[head], (8, rows))


def pair_kernel(kept_ref, received_ref, packed_ref):
    rows = kept_ref.shape[1]
    pieces = rows // PIECE
    total_row = slice(HEAD_SIZE, HEAD_SIZE + 1)
    max_row = slice(HEAD_SIZE + 8, HEAD_SIZE + 9)
    peak = jnp.maximum(kept_ref[max_row], received_ref[max_row])
    peak = peak.astype(jnp.bfloat16).astype(jnp.float32)
    kept_factor = jnp.exp2(kept_ref[max_row] - peak)
    received_factor = jnp.exp2(received_ref[max_row] - peak)
    total = kept_ref[total_row] * kept_factor + received_ref[total_row] * received_factor
    out = (
        kept_ref[:HEAD_SIZE] * (kept_factor / total)
        + received_ref[:HEAD_SIZE] * (received_factor / total)
    ).T.astype(jnp.bfloat16)
    high = total.astype(jnp.bfloat16).astype(jnp.float32)
    row = lax.broadcasted_iota(jnp.int32, (pieces, PIECE, HEAD_SIZE), 1)
    lane = lax.broadcasted_iota(jnp.int32, (pieces, PIECE, HEAD_SIZE), 2)

    def spread(value):
        return jnp.broadcast_to(value, (HEAD_SIZE, rows)).T.reshape(pieces, PIECE, HEAD_SIZE)

    stats = jnp.where(lane == row, spread(peak), 0.0)
    stats = jnp.where(lane == row + PIECE, spread(high), stats)
    stats = jnp.where(lane == row + 2 * PIECE, spread(total - high), stats)
    stats = jnp.sum(stats, axis=1, keepdims=True).astype(jnp.bfloat16)
    packed_ref[:, :PIECE] = out.reshape(pieces, PIECE, HEAD_SIZE)
    packed_ref[:, PIECE:] = jnp.broadcast_to(stats, (pieces, 8, HEAD_SIZE))


def repeat_kernel(value_ref, copies_ref):
    copies_ref[...] = jnp.broadcast_to(value_ref[...][None], copies_ref.shape)


def merge_kernel(packed_ref, attended_ref):
    chips = packed_ref.shape[0]
    stats = jnp.max(packed_ref[:, PIECE:].astype(jnp.float32), axis=1).T
    row_max = stats[:PIECE]
    totals = stats[PIECE : 2 * PIECE] + stats[2 * PIECE : 3 * PIECE]
    peak = jnp.max(row_max, axis=1, keepdims=True)
    shares = totals * jnp.exp2(row_max - peak)
    shares = shares / jnp.sum(shares, axis=1, keepdims=True)
    merged = jnp.zeros(attended_ref.shape[1:], jnp.float32)
    for chip in range(chips):
        merged += shares[:, chip : chip + 1] * packed_ref[chip, :PIECE].astype(jnp.float32)
    attended_ref[...] = jnp.broadcast_to(merged.astype(jnp.bfloat16)[None], attended_ref.shape)


def project_kernel(own_ref, sibling_ref, weight_ref, out_ref):
    my_core = lax.axis_index("hst") % CORES
    groups = out_ref.shape[0]
    heads = own_ref.shape[0] // groups
    depth = heads * HEAD_SIZE
    total = jnp.zeros((groups * PIECE, out_ref.shape[2]), jnp.float32)
    for source, core in ((own_ref, my_core), (sibling_ref, 1 - my_core)):
        lhs = jnp.concatenate(
            [
                source[head * groups : (head + 1) * groups].reshape(-1, HEAD_SIZE)
                for head in range(heads)
            ],
            axis=1,
        )
        total += dot(lhs, weight_ref[pl.ds(pl.multiple_of(core * depth, depth), depth)], 1, 0)
    out_ref[...] = total.reshape(out_ref.shape)


def sum_kernel(*refs):
    *part_refs, out_ref = refs
    out_ref[...] = sum(part_ref[...] for part_ref in part_refs).astype(out_ref.dtype)


def kernel_call(body, out_shape, in_specs, scratch=(), vmem=40, name=None):
    return pl.pallas_call(
        body,
        out_shape=out_shape,
        in_specs=in_specs,
        out_specs=jax.tree.map(lambda _: VMEM, out_shape),
        scratch_shapes=scratch,
        compiler_params=pltpu.CompilerParams(vmem_limit_bytes=vmem << 20),
        name=name,
    )


def shift(value, dz, dx, dcore):
    def index(z, x, core):
        return ((z % Z) * X + x % X) * CORES + core % CORES

    pairs = [
        (index(z, x, core), index(z + dz, x + dx, core + dcore))
        for z in range(Z)
        for x in range(X)
        for core in range(CORES)
    ]
    return lax.ppermute(value, "hst", pairs)


def gather(value, groups):
    copies = jnp.broadcast_to(value[None], (len(groups[0]), *value.shape))
    return lax.all_to_all(copies, "hst", 0, 0, axis_index_groups=groups)


def broadcast_queries(slots, root, ready):
    me = lax.axis_index("hst")
    core, x = me % CORES, me // CORES % X
    root_core, root_x, root_z = root % CORES, root // CORES % X, root // (CORES * X)
    tokens, width = slots.shape
    part = width // CORES
    own = lax.optimization_barrier(lax.dynamic_slice_in_dim(slots, core * part, part, 1))
    other = lax.dynamic_slice_in_dim(shift(slots, 0, 0, 1), core * part, part, 1)
    half = jnp.where(core == root_core, own, other).reshape(X, tokens // X, part)

    group = lax.dynamic_index_in_dim(half, x, 0, keepdims=False)
    for hop in range(1, X):
        sent = lax.dynamic_index_in_dim(half, (x + hop) % X, 0, keepdims=False)
        group = jnp.where((x - root_x) % X == hop, shift(sent, 0, hop, 0), group)

    columns = [[(z * X + i) * CORES + c for z in range(Z)] for i in range(X) for c in range(CORES)]
    group = lax.dynamic_index_in_dim(gather(group, columns), root_z, 0, keepdims=False)
    group, ready = lax.optimization_barrier((group, ready))

    half = jnp.stack([group] + [shift(group, 0, hop, 0) for hop in range(1, X)])
    return half, shift(half, 0, 0, 1), ready


def on_device(query_slots, keys, values, counts, query_host, out_weight):
    tokens, width = query_slots.shape[1:]
    kv_heads = keys.shape[1] // HEAD_SIZE
    rows = width // keys.shape[1] * tokens
    pieces = rows // PIECE
    root = query_host[0]
    me = lax.axis_index("hst")

    with jax.named_scope("queries"):
        last = counts[0]
        first = jnp.where(me == root, last - tokens + 1, last)
        scalars = jnp.stack([first, last, me % CORES, me // CORES % X])
        own, other, ready = broadcast_queries(
            query_slots[0], root, (scalars, keys[:CHUNK], values[:CHUNK])
        )
        scalars, keys_start, values_start = ready

    with jax.named_scope("attend"):
        result = jax.ShapeDtypeStruct((HEAD_SIZE + 16, rows), jnp.float32)
        kept, sent = kernel_call(
            attend_kernel,
            (result, result),
            [SMEM, VMEM, VMEM, VMEM, VMEM, HBM, HBM],
            [
                pltpu.VMEM((kv_heads, rows, HEAD_SIZE), jnp.bfloat16),
                pltpu.VMEM(keys.shape, jnp.bfloat16),
                pltpu.VMEM(values.shape, jnp.bfloat16),
                pltpu.VMEM((kv_heads, 1, rows), jnp.float32),
                pltpu.SemaphoreType.DMA((2, len(STAGES))),
            ],
            vmem=51,
            name="attend",
        )(scalars, own, other, keys_start, values_start, keys, values)

    with jax.named_scope("merge"):
        packed = kernel_call(
            pair_kernel,
            jax.ShapeDtypeStruct((pieces, PIECE + 8, HEAD_SIZE), jnp.bfloat16),
            [VMEM, VMEM],
            name="pair",
        )(kept, shift(sent, 0, 0, 1))
        chips = [[chip * CORES + core for chip in range(Z * X)] for core in range(CORES)]
        packed = lax.all_to_all(packed, "hst", 0, 0, axis_index_groups=chips)
        attended = kernel_call(
            merge_kernel,
            jax.ShapeDtypeStruct((pieces, PIECE, HEAD_SIZE), jnp.bfloat16),
            [VMEM],
            name="merge",
        )(packed)
        attended = lax.all_to_all(attended, "hst", 0, 0, axis_index_groups=chips)

    with jax.named_scope("project"):
        projected = kernel_call(
            project_kernel,
            jax.ShapeDtypeStruct((tokens // PIECE, PIECE, out_weight.shape[1]), jnp.float32),
            [VMEM] * 3,
            name="project",
        )(attended, shift(attended, 0, 0, 1), out_weight)
        shares = lax.axis_size("tensor")
        mine = lax.axis_index("tensor")
        parts = [lax.dynamic_index_in_dim(projected, mine, 0, keepdims=False)]
        for hop in range(1, shares):
            part = lax.dynamic_index_in_dim(projected, (mine + hop) % shares, 0, keepdims=False)
            parts.append(
                lax.ppermute(part, "tensor", [(k, (k + hop) % shares) for k in range(shares)])
            )
        return kernel_call(
            sum_kernel,
            jax.ShapeDtypeStruct(parts[0].shape, jnp.bfloat16),
            [VMEM] * shares,
            name="sum",
        )(*parts)


def solution(mesh):
    placed = (
        P("hst", None, "tensor"),
        P("hst", "tensor"),
        P("hst", "tensor"),
        P("hst"),
        P(),
        P("tensor", "hst"),
    )
    return jax.shard_map(
        on_device, mesh=mesh, in_specs=placed, out_specs=P("tensor", "hst"), check_vma=False
    )
```
